32 devices in a mesh: grp: 2 (over y), exp: 4 (over z), wsh: 4 (over x, core).
Axes of the slice: x: 2, y: 2, z: 4, core: 2. Of those that a mesh axis runs over, the one named last changes fastest.
Arguments:
- hidden_in: bfloat16 [4096, 2880], P(('grp', 'exp', 'wsh')), parts along dimension 0
- norm_gain: float32 [2880], replicated, may hold values from 0.1 to 1.9
- expert_ids: int32 [4096, 4], P(('grp', 'exp', 'wsh')), parts along dimension 0, may hold values from 0 to 3, as said below
- gate_weights: bfloat16 [4096, 4], P(('grp', 'exp', 'wsh')), parts along dimension 0, may hold values from 0.049804688 to 1
- gate_up_codes: bfloat16 [4, 2880, 2880], P('exp', None, 'wsh'), may hold values from -6 to 6
- gate_up_scales: int32 [4, 90, 2880], P('exp', None, 'wsh'), may hold values from 7 to 9
- down_codes: bfloat16 [4, 1440, 2880], P('exp', None, 'wsh'), may hold values from -6 to 6
- down_scales: int32 [4, 45, 2880], P('exp', None, 'wsh'), may hold values from 6 to 8
Outputs:
- mixture: bfloat16 [4096, 2880], P(('grp', 'exp', 'wsh')), parts along dimension 0
The draws below stay inside these ranges and needn't reach their ends.
There are 2 independent parts, one for each index of `grp`. The reference program is written for one: setup_inputs(seed, part) draws one part's arguments, and reference() takes and returns one part's arrays. A program takes and returns all parts, laid end to end along the dimension named above; an argument that names none is the same for every part. Nothing has to cross between parts.
Inputs may be any that keep to these rules, and one draw needn't show every extreme that they name: `expert_ids`: each row names 4 different experts; one expert, drawn anew in each draw, is named by every token, so it fills all 64 rows from every block.
All inputs are finite; a program needn't handle non-finite values.
Results may differ from the reference program's by a relative error of at most 0.0067.
Values may be sent and summed in bfloat16 or wider, within the bound.
A program may use at most 128 MiB of HBM per device.

```python
import math
import jax
import jax.numpy as jnp
from jax import lax

D = 2880
FF = 1440
TOP = 4
BLOCK = 32
TOK_DEV = 128
EXPERTS = 4
CAP = 64
TOKENS = 2048


def draw_expert_ids(key, part):
    key = jax.random.fold_in(key, 5)
    hot_key, score_key, lean_key = jax.random.split(key, 3)
    blocks = TOKENS // TOK_DEV
    hot_expert = jax.random.randint(hot_key, (), 0, EXPERTS)
    noise_part = jax.random.randint(score_key, (TOKENS, EXPERTS), 0, 4096)
    block_lean = jax.random.randint(lean_key, (blocks, EXPERTS), 0, 2048)
    block_lean = jnp.repeat(block_lean, TOK_DEV, axis=0)
    labels = jnp.arange(EXPERTS, dtype=jnp.int32)
    scores = (noise_part + block_lean + jnp.where(labels == hot_expert, 8192, 0)) * EXPERTS + labels
    return lax.top_k(scores, TOP)[1].astype(jnp.int32)


def draw_hidden_in(key, part):
    key = jax.random.fold_in(key, 11)
    row_key, col_key, val_key = jax.random.split(key, 3)
    row_scale = jnp.exp(jax.random.uniform(row_key, (TOKENS, 1), jnp.float32, 0.0, math.log(10.0)))
    col_scale = jnp.exp(jax.random.uniform(col_key, (1, D), jnp.float32, 0.0, math.log(10.0)))
    values = jax.random.normal(val_key, (TOKENS, D), jnp.float32)
    return (0.3 * values * row_scale * col_scale).astype(jnp.bfloat16)


def plant(drawn, key, least, high):
    dims = drawn.shape
    index_at = [jax.random.randint(jax.random.fold_in(key, axis), (), 0, dims[axis]) for axis in range(len(dims))]
    drawn = drawn.at[tuple(index_at)].set(least)
    longest = dims.index(max(dims))
    index_at[longest] = (index_at[longest] + 1) % dims[longest]
    return drawn.at[tuple(index_at)].set(high)


def level_of(rng, extent, shards, low, largest):
    loudness, own = 1.0, jax.random.fold_in(rng, 6)
    for position, blocks in shards:
        heights = jnp.exp(jax.random.uniform(jax.random.fold_in(own, position), (blocks,), jnp.float32, low / len(shards), largest / len(shards)))
        loudness = loudness * jnp.repeat(heights, extent[position] // blocks).reshape([-1 if axis == position else 1 for axis in range(len(extent))])
    return loudness


def setup_inputs(seed: int = 0, part: int = 0) -> dict:
    seeds = jax.random.split(jax.random.key(seed), 9)
    own_keys = jax.random.split(jax.random.fold_in(seeds[8], part), 9)
    return {
        "hidden_in": draw_hidden_in(jax.random.fold_in(jax.random.fold_in(seeds[8], part), 71), part),
        "norm_gain": jnp.clip(1.0 + 0.18 * jax.random.normal(seeds[1], (D,), jnp.float32), 0.1, 1.9),
        "expert_ids": draw_expert_ids(jax.random.fold_in(jax.random.fold_in(seeds[8], part), 71), part),
        "gate_weights": jnp.clip(0.049804688 + 0.9501953 * jax.random.uniform(own_keys[3], (TOKENS, TOP), jnp.float32) ** level_of(own_keys[3], (TOKENS, TOP), ((0, 16),), -0.2, 0.2), 0.049804688, 1.0).astype(jnp.bfloat16),
        "gate_up_codes": jnp.clip(jax.random.uniform(seeds[4], (EXPERTS, D, 2 * FF), jnp.float32, -6.0, 6.0) * level_of(seeds[4], (EXPERTS, D, 2 * FF), ((0, 4), (2, 4)), -0.4, 0.0), -6.0, 6.0).astype(jnp.bfloat16),
        "gate_up_scales": plant(jax.random.randint(seeds[5], (EXPERTS, D // BLOCK, 2 * FF), 7, 10), jax.random.fold_in(seeds[5], 1), 7, 9).astype(jnp.int32),
        "down_codes": jnp.clip(jax.random.uniform(seeds[6], (EXPERTS, FF, D), jnp.float32, -6.0, 6.0) * level_of(seeds[6], (EXPERTS, FF, D), ((0, 4), (2, 4)), -0.4, 0.0), -6.0, 6.0).astype(jnp.bfloat16),
        "down_scales": plant(jax.random.randint(seeds[7], (EXPERTS, FF // BLOCK, D), 6, 9), jax.random.fold_in(seeds[7], 1), 6, 8).astype(jnp.int32),
    }


EPSILON = 1e-05
SWISH_ALPHA = 1.702

def normalize(hidden_in, norm_gain):
    values = hidden_in.astype(jnp.float32)
    meansq = lax.optimization_barrier(jnp.mean(values * values, axis=-1, keepdims=True))
    return (values * lax.rsqrt(meansq + EPSILON) * norm_gain).astype(jnp.bfloat16)

def expand_block(mantissa, exponent):
    groups = exponent.shape[-2]
    factor = jnp.exp2(-exponent.astype(jnp.float32)).astype(jnp.bfloat16)
    shaped = mantissa.reshape(mantissa.shape[:-2] + (groups, mantissa.shape[-2] // groups, mantissa.shape[-1]))
    return (shaped * factor[..., :, None, :]).reshape(mantissa.shape)

def activate(gate_up, inner_width):
    gate_part = gate_up[:, :inner_width]
    upward = gate_up[:, inner_width:]
    return ((upward + 1.0) * gate_part * jax.nn.sigmoid(SWISH_ALPHA * gate_part)).astype(jnp.bfloat16)

def block_slots(block_ids, expert_count, capacity):
    rows, picks = block_ids.shape
    labels = jnp.arange(expert_count, dtype=jnp.int32)
    onehot = (block_ids.reshape(rows * picks)[:, None] == labels[None, :]).astype(jnp.int32)
    earlier = jnp.cumsum(onehot, axis=0) - onehot
    ranking = lax.optimization_barrier(jnp.sum(earlier * onehot, axis=1)).reshape(rows, picks)
    return jnp.where(ranking < capacity, ranking, -1).astype(jnp.int32)

def reference(hidden_in, norm_gain, expert_ids, gate_weights, gate_up_codes, gate_up_scales, down_codes, down_scales):
    normed = normalize(hidden_in, norm_gain)
    blocks = TOKENS // TOK_DEV
    places = EXPERTS * CAP
    slot_index = jax.vmap(lambda ids: block_slots(ids, EXPERTS, CAP))(expert_ids.reshape(blocks, TOK_DEV, TOP))
    slot_index = slot_index.reshape(TOKENS, TOP)
    target = jnp.where(slot_index >= 0, expert_ids * CAP + slot_index, places).astype(jnp.int32)
    target = target.reshape(blocks, TOK_DEV, TOP)
    source = jnp.broadcast_to(jnp.arange(blocks, dtype=jnp.int32)[:, None], (blocks, TOK_DEV))
    token_rows = normed.reshape(blocks, TOK_DEV, D)
    buffer = jnp.zeros((blocks, places, D), normed.dtype)
    for choice_slot in range(TOP):
        buffer = buffer.at[source, target[:, :, choice_slot]].set(token_rows, mode='drop')
    grouped = buffer.reshape(blocks, EXPERTS, CAP, D).transpose(1, 0, 2, 3).reshape(EXPERTS, blocks * CAP, D)

    def one_expert(members):
        expert_in, first_codes, first_scales, second_codes, second_scales = members
        gate_up = jnp.dot(expert_in, expand_block(first_codes, first_scales), preferred_element_type=jnp.float32)
        hidden_act = activate(gate_up, FF)
        return jnp.dot(hidden_act, expand_block(second_codes, second_scales), preferred_element_type=jnp.float32).astype(jnp.bfloat16)
    results = lax.map(one_expert, (grouped, gate_up_codes, gate_up_scales, down_codes, down_scales))
    results = results.reshape(EXPERTS, blocks, CAP, D).transpose(1, 0, 2, 3).reshape(blocks, places, D)
    weights_all = gate_weights.reshape(blocks, TOK_DEV, TOP).astype(jnp.float32)
    mixture = jnp.zeros((blocks, TOK_DEV, D), jnp.float32)
    for choice_slot in range(TOP):
        column = target[:, :, choice_slot]
        clipped = jnp.minimum(column, places - 1)
        picked = results[source, clipped].astype(jnp.float32)
        weighting = jnp.where(column < places, weights_all[:, :, choice_slot], jnp.zeros((), jnp.float32))
        mixture = mixture + weighting[:, :, None] * picked
    return mixture.reshape(TOKENS, D).astype(jnp.bfloat16)
```

```python
import jax
import jax.numpy as jnp
from jax import lax
from jax.experimental import pallas as pl
from jax.experimental.pallas import tpu as pltpu
from jax.sharding import PartitionSpec as P

EPSILON = 1e-05
SWISH_ALPHA = 1.702


def normalize(hidden_in, norm_gain):
    values = hidden_in.astype(jnp.float32)
    meansq = jnp.mean(values * values, axis=-1, keepdims=True)
    return (values * lax.rsqrt(meansq + EPSILON) * norm_gain).astype(jnp.bfloat16)


def expand_block(mantissa, exponent):
    groups = exponent.shape[-2]
    factor = jnp.exp2(-exponent.astype(jnp.float32)).astype(jnp.bfloat16)
    shaped = mantissa.reshape(
        mantissa.shape[:-2] + (groups, mantissa.shape[-2] // groups, mantissa.shape[-1])
    )
    return (shaped * factor[..., :, None, :]).reshape(mantissa.shape)


def activate(gate_up, inner_width):
    gate_part = gate_up[:, :inner_width]
    upward = gate_up[:, inner_width:]
    return ((upward + 1.0) * gate_part * jax.nn.sigmoid(SWISH_ALPHA * gate_part)).astype(
        jnp.bfloat16
    )


def block_slots(block_ids, expert_count, capacity):
    rows, picks = block_ids.shape
    labels = jnp.arange(expert_count, dtype=jnp.int32)
    onehot = (block_ids.reshape(rows * picks)[:, None] == labels[None, :]).astype(jnp.int32)
    earlier = jnp.cumsum(onehot, axis=0) - onehot
    ranking = jnp.sum(earlier * onehot, axis=1).reshape(rows, picks)
    return jnp.where(ranking < capacity, ranking, -1)


def per_device(
    hidden_in,
    norm_gain,
    expert_ids,
    gate_weights,
    gate_up_codes,
    gate_up_scales,
    down_codes,
    down_scales,
):
    normed = normalize(hidden_in, norm_gain)
    tok_rows, model_width = hidden_in.shape
    picks_per = expert_ids.shape[1]
    owners = lax.axis_size("exp")
    capacity = min(tok_rows // 2, tok_rows * picks_per // owners)
    slot_index = block_slots(expert_ids, owners, capacity)
    target = jnp.where(slot_index >= 0, expert_ids * capacity + slot_index, -1)
    positions = jnp.arange(owners * capacity, dtype=jnp.int32)
    matches = target[:, :, None] == positions[None, None, :]
    placing = jnp.any(matches, axis=1).astype(jnp.bfloat16)
    outgoing = jnp.einsum("ts,td->sd", placing, normed, preferred_element_type=jnp.float32).astype(
        jnp.bfloat16
    )
    outgoing = outgoing.reshape(owners, capacity, model_width)
    inner_width = down_codes.shape[1]
    arrived = lax.all_to_all(outgoing, "exp", split_axis=0, concat_axis=0, tiled=True)
    arrived = arrived.reshape(owners * capacity, model_width)
    shard_piece = lax.all_gather((gate_up_codes[0], gate_up_scales[0]), "wsh", axis=1, tiled=True)
    gate_up = jnp.dot(
        arrived, expand_block(shard_piece[0], shard_piece[1]), preferred_element_type=jnp.float32
    )
    hidden_act = activate(gate_up, inner_width)
    shard_piece = lax.all_gather((down_codes[0], down_scales[0]), "wsh", axis=1, tiled=True)
    expert_out = jnp.dot(
        hidden_act, expand_block(shard_piece[0], shard_piece[1]), preferred_element_type=jnp.float32
    )
    expert_rows = expert_out.astype(jnp.bfloat16).reshape(owners, capacity, model_width)
    came_back = lax.all_to_all(expert_rows, "exp", split_axis=0, concat_axis=0, tiled=True).reshape(
        owners * capacity, model_width
    )
    weighting = jnp.sum(
        jnp.where(matches, gate_weights[:, :, None], jnp.zeros((), jnp.bfloat16)), axis=1
    )
    mixture = jnp.dot(weighting, came_back, preferred_element_type=jnp.float32)
    return mixture.astype(jnp.bfloat16)


MESH = pl.DeviceIdType.MESH
TILE = 256
GROUP = 32


def fused_kernel(
    hid, gain, ids, gates, guc, gus, dnc, dns, out,
    stage_g, stage_d, fac_g, fac_d, wg, wd, nrm, weighting, og, xb, first, act, res, back,
    load_sem, xs, xr, ys, yr, zs, zr, cs, cr, act_s, act_r, rs, rr,
):
    grp = lax.axis_index("grp")
    z = lax.axis_index("exp")
    w = lax.axis_index("wsh")
    x = w // 2
    c = w % 2
    slot = z * 2 + c
    mate = x * 2 + (1 - c)
    across = (1 - x) * 2 + c
    depth, width = stage_g.shape
    inner = stage_d.shape[0]
    half_g, half_d = depth // 2, inner // 2
    step_g, step_d = half_g // 3, half_d // 3
    tokens = hid.shape[0]
    cap = og.shape[1]

    loads = []
    for k in range(2):
        part = (grp + k) % 2
        rows = pl.ds(pl.multiple_of(part * half_g, 16), half_g)
        loads.append(pltpu.make_async_copy(guc.at[0, rows], stage_g.at[rows], load_sem.at[k]))
    loads.append(pltpu.make_async_copy(dnc.at[0], stage_d, load_sem.at[2]))
    for load in loads:
        load.start()

    barrier = pltpu.get_barrier_semaphore()
    pl.semaphore_signal(barrier, inc=1, device_id={"wsh": across}, device_id_type=MESH)
    pl.semaphore_signal(barrier, inc=1, device_id={"grp": 1 - grp}, device_id_type=MESH)
    for d in range(1, 8):
        other = (slot + d) % 8
        pl.semaphore_signal(
            barrier, inc=1, device_id={"exp": other // 2, "wsh": x * 2 + other % 2}, device_id_type=MESH
        )

    fac_g[...] = jnp.exp2(-gus[0].astype(jnp.float32))
    fac_d[...] = jnp.exp2(-dns[0].astype(jnp.float32))
    wg[0, 2] = jnp.zeros((depth, TILE), jnp.bfloat16)
    wd[0, 2] = jnp.zeros((inner, TILE), jnp.bfloat16)

    def expand(stage, fac, dest, j, start, groups):
        lanes = min(TILE, width - j * TILE)

        @pl.loop(0, groups)
        def _(g):
            at = start + g
            row = pl.multiple_of(at * GROUP, GROUP)
            scale = fac[pl.ds(at, 1), pl.ds(j * TILE, lanes)]
            scale = jnp.broadcast_to(scale, (GROUP, lanes)).astype(jnp.bfloat16)
            dest[0, j, pl.ds(row, GROUP), pl.ds(0, lanes)] = (
                stage[pl.ds(row, GROUP), pl.ds(j * TILE, lanes)] * scale
            )

    def place(i):
        buf = wg if i < 9 else wd
        j, s = (i % 9) // 3, i % 3
        return buf, j, s, (half_g if i < 9 else half_d), (step_g if i < 9 else step_d)

    def x_copy(i):
        buf, j, s, half, step = place(i)
        rows = pl.ds(pl.multiple_of(grp * half + s * step, 16), step)
        return pltpu.make_async_remote_copy(
            src_ref=buf.at[0, j, rows], dst_ref=buf.at[1, j, rows], send_sem=xs.at[i], recv_sem=xr.at[i],
            device_id={"wsh": across}, device_id_type=MESH,
        )

    def y_copy(i, side=None):
        buf, j, s, half, step = place(i)
        side = grp if side is None else side
        rows = pl.ds(pl.multiple_of(side * half + s * step, 16), step)
        return pltpu.make_async_remote_copy(
            src_ref=buf.at[1, j, rows], dst_ref=buf.at[1, j, rows], send_sem=ys.at[i], recv_sem=yr.at[i],
            device_id={"grp": 1 - grp}, device_id_type=MESH,
        )

    def forward(i):
        x_copy(i).wait_recv()
        y_copy(i).start()

    loads[0].wait()
    per = step_g // GROUP
    for j in range(3):
        for s in range(3):
            expand(stage_g, fac_g, wg, j, grp * (half_g // GROUP) + s * per, per)
            if j == 0 and s == 0:
                pl.semaphore_wait(barrier, 9)
            x_copy(j * 3 + s).start()

    @pl.loop(0, tokens // 32)
    def _(b):
        rows = pl.ds(pl.multiple_of(b * 32, 32), 32)
        values = hid[rows, :].astype(jnp.float32)
        meansq = jnp.sum(values * values, axis=-1, keepdims=True) / depth
        nrm[rows, :] = (values * lax.rsqrt(meansq + EPSILON) * gain[...]).astype(jnp.bfloat16)

    picks = ids.shape[1]
    chosen = ids[...]
    gate_values = gates[...].astype(jnp.float32)
    label = lax.broadcasted_iota(jnp.int32, (tokens, 128), 1)
    named = jnp.zeros((tokens, 128), jnp.float32)
    for k in range(picks):
        named = named + jnp.where(chosen[:, k : k + 1] == label, 1.0, 0.0)
    row_at = lax.broadcasted_iota(jnp.int32, (tokens, tokens), 0)
    col_at = lax.broadcasted_iota(jnp.int32, (tokens, tokens), 1)
    earlier = jnp.where(col_at < row_at, 1.0, 0.0).astype(jnp.bfloat16)
    rank = jnp.dot(earlier, named.astype(jnp.bfloat16), preferred_element_type=jnp.float32)
    blocks = []
    weights = []
    lane = lax.broadcasted_iota(jnp.int32, (tokens, 128), 1)
    for pair in range(2):
        expert = jnp.where(lane < cap, 2 * pair, 2 * pair + 1)
        position = jnp.where(lane < cap, lane, lane - cap).astype(jnp.float32)
        ranked = jnp.where(
            lane < cap, rank[:, 2 * pair : 2 * pair + 1], rank[:, 2 * pair + 1 : 2 * pair + 2]
        )
        hit = jnp.zeros((tokens, 128), jnp.float32)
        value = jnp.zeros((tokens, 128), jnp.float32)
        for k in range(picks):
            same = chosen[:, k : k + 1] == expert
            hit = hit + jnp.where(same, 1.0, 0.0)
            value = value + jnp.where(same, gate_values[:, k : k + 1], 0.0)
        placed = jnp.where(ranked == position, hit, 0.0)
        blocks.append(placed.T.astype(jnp.bfloat16))
        weighting[:, pair * 128 : (pair + 1) * 128] = (placed * value).astype(jnp.bfloat16)
    for pair in range(2):
        rows = jnp.dot(blocks[pair], nrm[...], preferred_element_type=jnp.float32).astype(jnp.bfloat16)
        og[2 * pair] = rows[:cap]
        og[2 * pair + 1] = rows[cap:]

    def slot_rows(s):
        return pl.ds(pl.multiple_of(s * cap, 16), cap)

    def z_copy(d):
        to = (z + d) % 4
        return pltpu.make_async_remote_copy(
            src_ref=og.at[to], dst_ref=xb.at[slot_rows(slot)], send_sem=zs.at[d], recv_sem=zr.at[d],
            device_id={"exp": to}, device_id_type=MESH,
        )

    def z_arrived(d):
        frm = ((z + 4 - d) % 4) * 2 + c
        pltpu.make_async_remote_copy(
            src_ref=og.at[0], dst_ref=xb.at[slot_rows(frm)], send_sem=zs.at[d], recv_sem=zr.at[d],
            device_id={"exp": (z + d) % 4}, device_id_type=MESH,
        ).wait_recv()

    def c_copy(d, core=None):
        core = c if core is None else core
        rows = slot_rows(((z + 4 - d) % 4) * 2 + core)
        return pltpu.make_async_remote_copy(
            src_ref=xb.at[rows], dst_ref=xb.at[rows], send_sem=cs.at[d], recv_sem=cr.at[d],
            device_id={"wsh": mate}, device_id_type=MESH,
        )

    for d in (2, 1, 3):
        z_copy(d).start()
    xb[slot_rows(slot), :] = og[z]
    c_copy(0).start()

    loads[2].wait()
    for j in range(3):
        expand(stage_d, fac_d, wd, j, 0, inner // GROUP)
        for s in range(3):
            x_copy(9 + j * 3 + s).start()
    loads[1].wait()
    for j in range(3):
        expand(stage_g, fac_g, wg, j, (1 - grp) * (half_g // GROUP), half_g // GROUP)

    forward(0)
    forward(1)
    forward(2)
    z_arrived(1)
    c_copy(1).start()
    z_arrived(3)
    c_copy(3).start()
    forward(3)
    z_arrived(2)
    c_copy(2).start()
    forward(4)
    for d in range(4):
        c_copy(d, 1 - c).wait_recv()
    for j in range(3):
        first[j] = jnp.dot(xb[...], wg[0, j], preferred_element_type=jnp.float32)
        forward(5 + j)
    forward(8)

    rows_all = xb.shape[0]
    for j in range(3):
        for s in range(3):
            y_copy(j * 3 + s, 1 - grp).wait_recv()
        second = jnp.dot(xb[...], wg[1, j], preferred_element_type=jnp.float32)
        mine = first[j]
        gate = jnp.where(x == 0, mine, second)
        up = jnp.where(x == 0, second, mine)
        done = ((up + 1.0) * gate * jax.nn.sigmoid(SWISH_ALPHA * gate)).astype(jnp.bfloat16)
        lanes = min(TILE, width - j * TILE)
        act[c, :, j * TILE : j * TILE + lanes] = done[:, :lanes]

    def a_copy(core):
        return pltpu.make_async_remote_copy(
            src_ref=act.at[core], dst_ref=act.at[core], send_sem=act_s, recv_sem=act_r,
            device_id={"wsh": mate}, device_id_type=MESH,
        )

    a_copy(c).start()
    forward(9)
    forward(10)
    a_copy(1 - c).wait_recv()

    def quarter(h, core):
        return (x if h == 0 else 1 - x) * 2 + core

    def r_copy(h, j, d):
        other = (slot + d) % 8
        q = quarter(h, c)
        return pltpu.make_async_remote_copy(
            src_ref=res.at[h, j, slot_rows(other)], dst_ref=back.at[q, j, slot_rows(z)],
            send_sem=rs.at[h, j, d], recv_sem=rr.at[q, j, z],
            device_id={"exp": other // 2, "wsh": x * 2 + other % 2}, device_id_type=MESH,
        )

    def project(h, j):
        total = jnp.dot(act[0], wd[h, j, :half_d], preferred_element_type=jnp.float32)
        total = total + jnp.dot(act[1], wd[h, j, half_d:], preferred_element_type=jnp.float32)
        res[h, j] = total.astype(jnp.bfloat16)
        for d in (4, 5, 2, 3, 6, 7, 1):
            r_copy(h, j, d).start()
        back[quarter(h, c), j, slot_rows(z), :] = res[h, j, slot_rows(slot), :]

    def combine(h, j):
        for core in range(2):
            q = quarter(h, core)
            for e in range(4):
                @pl.when(jnp.logical_or(core != c, e != z))
                def _():
                    pltpu.make_async_remote_copy(
                        src_ref=res.at[h, j, slot_rows(0)], dst_ref=back.at[q, j, slot_rows(e)],
                        send_sem=rs.at[h, j, 1], recv_sem=rr.at[q, j, e],
                        device_id={"wsh": mate}, device_id_type=MESH,
                    ).wait_recv()
            out[q, :, j * TILE : (j + 1) * TILE] = jnp.dot(
                weighting[...], back[q, j], preferred_element_type=jnp.float32
            ).astype(jnp.bfloat16)

    project(0, 0)
    forward(11)
    project(0, 1)
    forward(12)
    project(0, 2)
    forward(13)
    for j in range(3):
        for i in range(14 + 3 * j, min(17 + 3 * j, 18)):
            forward(i)
        for s in range(3):
            y_copy(9 + j * 3 + s, 1 - grp).wait_recv()
        project(1, j)
        if j > 0:
            combine(0, j - 1)
    combine(0, 2)
    for j in range(3):
        combine(1, j)

    for i in range(18):
        x_copy(i).wait_send()
        y_copy(i).wait_send()
    for d in range(4):
        if d > 0:
            z_copy(d).wait_send()
        c_copy(d).wait_send()
    a_copy(c).wait_send()
    for h in range(2):
        for j in range(3):
            for d in range(1, 8):
                r_copy(h, j, d).wait_send()


def fused_device(
    hidden_in,
    norm_gain,
    expert_ids,
    gate_weights,
    gate_up_codes,
    gate_up_scales,
    down_codes,
    down_scales,
):
    tokens, depth = hidden_in.shape
    width = gate_up_codes.shape[2]
    inner = down_codes.shape[1]
    owners = lax.axis_size("exp")
    cap = min(tokens // 2, tokens * expert_ids.shape[1] // owners)
    rows = 2 * owners * cap
    vmem = pl.BlockSpec(memory_space=pltpu.VMEM)
    hbm = pl.BlockSpec(memory_space=pl.ANY)
    bf16, f32 = jnp.bfloat16, jnp.float32
    dma = pltpu.SemaphoreType.DMA
    tiles = pl.cdiv(width, TILE)
    out = pl.pallas_call(
        fused_kernel,
        out_shape=jax.ShapeDtypeStruct((4, tokens, tiles * TILE), bf16),
        in_specs=[vmem, vmem, vmem, vmem, hbm, vmem, hbm, vmem],
        out_specs=vmem,
        scratch_shapes=[
            pltpu.VMEM((depth, width), bf16),
            pltpu.VMEM((inner, width), bf16),
            pltpu.VMEM(gate_up_scales.shape[1:], f32),
            pltpu.VMEM(down_scales.shape[1:], f32),
            pltpu.VMEM((2, tiles, depth, TILE), bf16),
            pltpu.VMEM((2, tiles, inner, TILE), bf16),
            pltpu.VMEM((tokens, depth), bf16),
            pltpu.VMEM((tokens, owners * cap), bf16),
            pltpu.VMEM((owners, cap, depth), bf16),
            pltpu.VMEM((rows, depth), bf16),
            pltpu.VMEM((tiles, rows, TILE), f32),
            pltpu.VMEM((2, rows, width), bf16),
            pltpu.VMEM((2, tiles, rows, TILE), bf16),
            pltpu.VMEM((4, tiles, owners * cap, TILE), bf16),
            dma((3,)),
            dma((18,)), dma((18,)), dma((18,)), dma((18,)),
            dma((4,)), dma((4,)), dma((4,)), dma((4,)),
            dma, dma,
            dma((2, tiles, 8)), dma((4, tiles, owners)),
        ],
        compiler_params=pltpu.CompilerParams(
            collective_id=0, has_side_effects=True, vmem_limit_bytes=58 * 1024 * 1024
        ),
        name="moe_block",
    )(
        hidden_in,
        norm_gain.reshape(1, depth),
        expert_ids,
        gate_weights,
        gate_up_codes,
        gate_up_scales,
        down_codes,
        down_scales,
    )
    return jnp.concatenate([out[q, :, :width] for q in range(4)], axis=1)


def solution(mesh):
    placed = (
        P(("grp", "exp", "wsh"), None),
        P(),
        P(("grp", "exp", "wsh"), None),
        P(("grp", "exp", "wsh"), None),
        P("exp", None, "wsh"),
        P("exp", None, "wsh"),
        P("exp", None, "wsh"),
        P("exp", None, "wsh"),
    )
    body = per_device
    if mesh.shape["wsh"] == 4 and mesh.shape["exp"] == 4 and mesh.shape["grp"] == 2:
        body = fused_device
    return jax.shard_map(
        body,
        mesh=mesh,
        in_specs=placed,
        out_specs=P(("grp", "exp", "wsh"), None),
        check_vma=False,
    )
```

```python
import jax
import jax.numpy as jnp
from jax import lax
from jax.experimental import pallas as pl
from jax.experimental.pallas import tpu as pltpu
from jax.sharding import PartitionSpec as P

EPSILON = 1e-05
SWISH_ALPHA = 1.702


def normalize(hidden_in, norm_gain):
    values = hidden_in.astype(jnp.float32)
    meansq = jnp.mean(values * values, axis=-1, keepdims=True)
    return (values * lax.rsqrt(meansq + EPSILON) * norm_gain).astype(jnp.bfloat16)


def expand_block(mantissa, exponent):
    groups = exponent.shape[-2]
    factor = jnp.exp2(-exponent.astype(jnp.float32)).astype(jnp.bfloat16)
    shaped = mantissa.reshape(
        mantissa.shape[:-2] + (groups, mantissa.shape[-2] // groups, mantissa.shape[-1])
    )
    return (shaped * factor[..., :, None, :]).reshape(mantissa.shape)


def activate(gate_up, inner_width):
    gate_part = gate_up[:, :inner_width]
    upward = gate_up[:, inner_width:]
    return ((upward + 1.0) * gate_part * jax.nn.sigmoid(SWISH_ALPHA * gate_part)).astype(
        jnp.bfloat16
    )


def block_slots(block_ids, expert_count, capacity):
    rows, picks = block_ids.shape
    labels = jnp.arange(expert_count, dtype=jnp.int32)
    onehot = (block_ids.reshape(rows * picks)[:, None] == labels[None, :]).astype(jnp.int32)
    earlier = jnp.cumsum(onehot, axis=0) - onehot
    ranking = jnp.sum(earlier * onehot, axis=1).reshape(rows, picks)
    return jnp.where(ranking < capacity, ranking, -1)


def per_device(
    hidden_in,
    norm_gain,
    expert_ids,
    gate_weights,
    gate_up_codes,
    gate_up_scales,
    down_codes,
    down_scales,
):
    normed = normalize(hidden_in, norm_gain)
    tok_rows, model_width = hidden_in.shape
    picks_per = expert_ids.shape[1]
    owners = lax.axis_size("exp")
    capacity = min(tok_rows // 2, tok_rows * picks_per // owners)
    slot_index = block_slots(expert_ids, owners, capacity)
    target = jnp.where(slot_index >= 0, expert_ids * capacity + slot_index, -1)
    positions = jnp.arange(owners * capacity, dtype=jnp.int32)
    matches = target[:, :, None] == positions[None, None, :]
    placing = jnp.any(matches, axis=1).astype(jnp.bfloat16)
    outgoing = jnp.einsum("ts,td->sd", placing, normed, preferred_element_type=jnp.float32).astype(
        jnp.bfloat16
    )
    outgoing = outgoing.reshape(owners, capacity, model_width)
    inner_width = down_codes.shape[1]
    arrived = lax.all_to_all(outgoing, "exp", split_axis=0, concat_axis=0, tiled=True)
    arrived = arrived.reshape(owners * capacity, model_width)
    shard_piece = lax.all_gather((gate_up_codes[0], gate_up_scales[0]), "wsh", axis=1, tiled=True)
    gate_up = jnp.dot(
        arrived, expand_block(shard_piece[0], shard_piece[1]), preferred_element_type=jnp.float32
    )
    hidden_act = activate(gate_up, inner_width)
    shard_piece = lax.all_gather((down_codes[0], down_scales[0]), "wsh", axis=1, tiled=True)
    expert_out = jnp.dot(
        hidden_act, expand_block(shard_piece[0], shard_piece[1]), preferred_element_type=jnp.float32
    )
    expert_rows = expert_out.astype(jnp.bfloat16).reshape(owners, capacity, model_width)
    came_back = lax.all_to_all(expert_rows, "exp", split_axis=0, concat_axis=0, tiled=True).reshape(
        owners * capacity, model_width
    )
    weighting = jnp.sum(
        jnp.where(matches, gate_weights[:, :, None], jnp.zeros((), jnp.bfloat16)), axis=1
    )
    mixture = jnp.dot(weighting, came_back, preferred_element_type=jnp.float32)
    return mixture.astype(jnp.bfloat16)


MESH = pl.DeviceIdType.MESH
TILE = 256
GROUP = 32


def fused_kernel(
    hid, gain, ids, gates, guc, gus, dnc, dns, out,
    stage_g, stage_d, wg, wd, nrm, weighting, og, xb, first, act, res, back,
    load_sem, xs, xr, ys, yr, zs, zr, cs, cr, act_s, act_r, rs, rr,
):
    grp = lax.axis_index("grp")
    z = lax.axis_index("exp")
    w = lax.axis_index("wsh")
    x = w // 2
    c = w % 2
    slot = z * 2 + c
    mate = x * 2 + (1 - c)
    across = (1 - x) * 2 + c
    depth = stage_g.shape[1]
    inner, width = stage_d.shape
    half_g, half_d = depth // 2, inner // 2
    per_g, per_d = 6, 3
    step_g, step_d = half_g // per_g, half_d // per_d
    count_g = 3 * per_g
    count = count_g + 3 * per_d
    tokens = hid.shape[1]
    cap = og.shape[1]

    loads = []
    for j in range(3):
        rows = pl.ds(j * TILE, min(TILE, width - j * TILE))
        loads.append(pltpu.make_async_copy(guc.at[0, rows], stage_g.at[rows], load_sem.at[j]))
    loads.append(pltpu.make_async_copy(dnc.at[0], stage_d, load_sem.at[3]))
    for load in loads:
        load.start()

    barrier = pltpu.get_barrier_semaphore()
    pl.semaphore_signal(barrier, inc=1, device_id={"wsh": across}, device_id_type=MESH)
    pl.semaphore_signal(barrier, inc=1, device_id={"grp": 1 - grp}, device_id_type=MESH)
    for d in range(1, 8):
        other = (slot + d) % 8
        pl.semaphore_signal(
            barrier, inc=1, device_id={"exp": other // 2, "wsh": x * 2 + other % 2}, device_id_type=MESH
        )

    wg[0, 2] = jnp.zeros((depth, TILE), jnp.bfloat16)
    wd[0, 2] = jnp.zeros((inner, TILE), jnp.bfloat16)
    stage_g[width:, :] = jnp.zeros((stage_g.shape[0] - width, depth), jnp.bfloat16)

    def factor(scales, at, j, lanes):
        scale = jnp.exp2(-scales[at, :, pl.ds(j * TILE, lanes)].astype(jnp.float32))
        return jnp.broadcast_to(scale, (GROUP, lanes)).astype(jnp.bfloat16)

    def expand_down(j):
        lanes = min(TILE, width - j * TILE)

        @pl.loop(0, inner // GROUP)
        def _(g):
            row = pl.multiple_of(g * GROUP, GROUP)
            wd[0, j, pl.ds(row, GROUP), pl.ds(0, lanes)] = stage_d[
                pl.ds(row, GROUP), pl.ds(j * TILE, lanes)
            ] * factor(dns, g, j, lanes)

    def expand_gate_up(j):
        lanes = min(TILE, width - j * TILE)

        def block(at, extent):
            codes = stage_g[pl.ds(j * TILE, TILE), pl.ds(at, extent)].T
            for g in range(extent // GROUP):
                part = codes[g * GROUP : (g + 1) * GROUP, :lanes]
                scale = factor(gus, at // GROUP + g, j, lanes)
                wg[0, j, pl.ds(at + g * GROUP, GROUP), pl.ds(0, lanes)] = part * scale

        @pl.loop(0, depth // 128)
        def _(b):
            block(pl.multiple_of(b * 128, 128), 128)

        if depth % 128:
            block(depth // 128 * 128, depth % 128)

    def place(i):
        if i < count_g:
            return wg, i // per_g, i % per_g, half_g, step_g
        i = i - count_g
        return wd, i // per_d, i % per_d, half_d, step_d

    def x_copy(i):
        buf, j, s, half, step = place(i)
        rows = pl.ds(pl.multiple_of(grp * half + s * step, 16), step)
        return pltpu.make_async_remote_copy(
            src_ref=buf.at[0, j, rows], dst_ref=buf.at[1, j, rows], send_sem=xs.at[i], recv_sem=xr.at[i],
            device_id={"wsh": across}, device_id_type=MESH,
        )

    def y_copy(i, side=None):
        buf, j, s, half, step = place(i)
        side = grp if side is None else side
        rows = pl.ds(pl.multiple_of(side * half + s * step, 16), step)
        return pltpu.make_async_remote_copy(
            src_ref=buf.at[1, j, rows], dst_ref=buf.at[1, j, rows], send_sem=ys.at[i], recv_sem=yr.at[i],
            device_id={"grp": 1 - grp}, device_id_type=MESH,
        )

    def forward(i):
        x_copy(i).wait_recv()
        y_copy(i).start()

    for j in range(3):
        loads[j].wait()
        expand_gate_up(j)
        if j == 0:
            pl.semaphore_wait(barrier, 9)
        for s in range(per_g):
            x_copy(j * per_g + s).start()

    total = jnp.zeros((1, tokens), jnp.float32)
    for at in range(0, depth, 128):
        values = hid[at : min(at + 128, depth), :].astype(jnp.float32)
        total = total + jnp.sum(values * values, axis=0, keepdims=True)
    inverse = lax.rsqrt(total / depth + EPSILON)
    for at in range(0, depth, 128):
        end = min(at + 128, depth)
        values = (hid[at:end, :].astype(jnp.float32) * inverse).T
        nrm[:, at:end] = (values * gain[:, at:end]).astype(jnp.bfloat16)

    picks = ids.shape[0]
    owners = og.shape[0]
    chosen = ids[...]
    gate_values = gates[...].astype(jnp.float32)
    label = lax.broadcasted_iota(jnp.int32, (16, tokens), 0)
    named = jnp.zeros((16, tokens), jnp.float32)
    valued = jnp.zeros((16, tokens), jnp.float32)
    for k in range(picks):
        same = chosen[k : k + 1, :] == label
        named = named + jnp.where(same, 1.0, 0.0)
        valued = valued + jnp.where(same, gate_values[k : k + 1, :], 0.0)
    row_at = lax.broadcasted_iota(jnp.int32, (tokens, tokens), 0)
    col_at = lax.broadcasted_iota(jnp.int32, (tokens, tokens), 1)
    earlier = jnp.where(row_at < col_at, 1.0, 0.0).astype(jnp.bfloat16)
    rank = jnp.dot(named.astype(jnp.bfloat16), earlier, preferred_element_type=jnp.float32)
    position = lax.broadcasted_iota(jnp.int32, (cap, tokens), 0).astype(jnp.float32)
    placed = []
    for e in range(owners):
        hit = jnp.where(rank[e : e + 1, :] == position, named[e : e + 1, :], 0.0)
        placed.append(hit)
        og[e] = jnp.dot(
            hit.astype(jnp.bfloat16), nrm[...], preferred_element_type=jnp.float32
        ).astype(jnp.bfloat16)
    for pair in range(owners // 2):
        e = 2 * pair
        both = jnp.concatenate(
            [placed[e] * valued[e : e + 1, :], placed[e + 1] * valued[e + 1 : e + 2, :]], axis=0
        )
        weighting[:, 2 * cap * pair : 2 * cap * (pair + 1)] = both.T.astype(jnp.bfloat16)

    def slot_rows(s):
        return pl.ds(pl.multiple_of(s * cap, 16), cap)

    def z_copy(d):
        to = (z + d) % 4
        return pltpu.make_async_remote_copy(
            src_ref=og.at[to], dst_ref=xb.at[slot_rows(slot)], send_sem=zs.at[d], recv_sem=zr.at[d],
            device_id={"exp": to}, device_id_type=MESH,
        )

    def z_arrived(d):
        frm = ((z + 4 - d) % 4) * 2 + c
        pltpu.make_async_remote_copy(
            src_ref=og.at[0], dst_ref=xb.at[slot_rows(frm)], send_sem=zs.at[d], recv_sem=zr.at[d],
            device_id={"exp": (z + d) % 4}, device_id_type=MESH,
        ).wait_recv()

    def c_copy(d, core=None):
        core = c if core is None else core
        rows = slot_rows(((z + 4 - d) % 4) * 2 + core)
        return pltpu.make_async_remote_copy(
            src_ref=xb.at[rows], dst_ref=xb.at[rows], send_sem=cs.at[d], recv_sem=cr.at[d],
            device_id={"wsh": mate}, device_id_type=MESH,
        )

    for d in (2, 1, 3):
        z_copy(d).start()
    xb[slot_rows(slot), :] = og[z]
    c_copy(0).start()

    loads[3].wait()
    for j in range(3):
        expand_down(j)
        for s in range(per_d):
            x_copy(count_g + j * per_d + s).start()
    for i in range(12):
        forward(i)
    for d in (1, 3, 2):
        z_arrived(d)
        c_copy(d).start()
    forward(12)
    for d in range(4):
        c_copy(d, 1 - c).wait_recv()

    def a_copy(core, j):
        return pltpu.make_async_remote_copy(
            src_ref=act.at[core, j], dst_ref=act.at[core, j], send_sem=act_s.at[j], recv_sem=act_r.at[j],
            device_id={"wsh": mate}, device_id_type=MESH,
        )

    def activate_tile(j):
        for s in range(per_g):
            y_copy(j * per_g + s, 1 - grp).wait_recv()
        second = jnp.dot(xb[...], wg[1, j], preferred_element_type=jnp.float32)
        mine = first[j]
        gate = jnp.where(x == 0, mine, second)
        up = jnp.where(x == 0, second, mine)
        act[c, j] = ((up + 1.0) * gate * jax.nn.sigmoid(SWISH_ALPHA * gate)).astype(jnp.bfloat16)
        a_copy(c, j).start()

    for j in range(3):
        first[j] = jnp.dot(xb[...], wg[0, j], preferred_element_type=jnp.float32)
        forward(13 + j)
    activate_tile(0)
    forward(16)
    activate_tile(1)
    forward(17)
    activate_tile(2)
    forward(count_g)
    for j in range(3):
        a_copy(1 - c, j).wait_recv()

    def quarter(h, core):
        return (x if h == 0 else 1 - x) * 2 + core

    def r_copy(h, j, d):
        other = (slot + d) % 8
        q = quarter(h, c)
        return pltpu.make_async_remote_copy(
            src_ref=res.at[h, j, slot_rows(other)], dst_ref=back.at[q, j, slot_rows(z)],
            send_sem=rs.at[h, j, d], recv_sem=rr.at[q, j, z],
            device_id={"exp": other // 2, "wsh": x * 2 + other % 2}, device_id_type=MESH,
        )

    def project(h, j):
        total = jnp.zeros((act.shape[2], TILE), jnp.float32)
        for core in range(2):
            for k in range(3):
                lanes = min(TILE, width - k * TILE)
                at = core * half_d + k * TILE
                total = total + jnp.dot(
                    act[core, k, :, :lanes], wd[h, j, at : at + lanes], preferred_element_type=jnp.float32
                )
        res[h, j] = total.astype(jnp.bfloat16)
        for d in (4, 5, 2, 3, 6, 7, 1):
            r_copy(h, j, d).start()
        back[quarter(h, c), j, slot_rows(z), :] = res[h, j, slot_rows(slot), :]

    def combine(h, j):
        for core in range(2):
            q = quarter(h, core)
            for e in range(4):
                @pl.when(jnp.logical_or(core != c, e != z))
                def _():
                    pltpu.make_async_remote_copy(
                        src_ref=res.at[h, j, slot_rows(0)], dst_ref=back.at[q, j, slot_rows(e)],
                        send_sem=rs.at[h, j, 1], recv_sem=rr.at[q, j, e],
                        device_id={"wsh": mate}, device_id_type=MESH,
                    ).wait_recv()
            mixed = jnp.dot(weighting[...], back[q, j], preferred_element_type=jnp.float32)
            lanes = min(TILE, width - j * TILE)
            at = pl.multiple_of(q * width + j * TILE, 16)
            out[pl.ds(at, lanes), :] = mixed.T[:lanes].astype(jnp.bfloat16)

    project(0, 0)
    forward(count_g + 1)
    project(0, 1)
    forward(count_g + 2)
    project(0, 2)
    for j in range(3):
        for i in range(count_g + 3 + 3 * j, min(count_g + 6 + 3 * j, count)):
            forward(i)
        for s in range(per_d):
            y_copy(count_g + j * per_d + s, 1 - grp).wait_recv()
        project(1, j)
        if j > 0:
            combine(0, j - 1)
    combine(0, 2)
    for j in range(3):
        combine(1, j)

    for i in range(count):
        x_copy(i).wait_send()
        y_copy(i).wait_send()
    for d in range(4):
        if d > 0:
            z_copy(d).wait_send()
        c_copy(d).wait_send()
    for j in range(3):
        a_copy(c, j).wait_send()
    for h in range(2):
        for j in range(3):
            for d in range(1, 8):
                r_copy(h, j, d).wait_send()


def fused_device(
    hidden_in,
    norm_gain,
    expert_ids,
    gate_weights,
    gate_up_codes,
    gate_up_scales,
    down_codes,
    down_scales,
):
    tokens, depth = hidden_in.shape
    width = gate_up_codes.shape[2]
    inner = down_codes.shape[1]
    owners = lax.axis_size("exp")
    cap = min(tokens // 2, tokens * expert_ids.shape[1] // owners)
    rows = 2 * owners * cap
    vmem = pl.BlockSpec(memory_space=pltpu.VMEM)
    hbm = pl.BlockSpec(memory_space=pl.ANY)
    bf16, f32 = jnp.bfloat16, jnp.float32
    dma = pltpu.SemaphoreType.DMA
    tiles = pl.cdiv(width, TILE)
    out = pl.pallas_call(
        fused_kernel,
        out_shape=jax.ShapeDtypeStruct((depth, tokens), bf16),
        in_specs=[vmem, vmem, vmem, vmem, hbm, vmem, hbm, vmem],
        out_specs=vmem,
        scratch_shapes=[
            pltpu.VMEM((tiles * TILE, depth), bf16),
            pltpu.VMEM((inner, width), bf16),
            pltpu.VMEM((2, tiles, depth, TILE), bf16),
            pltpu.VMEM((2, tiles, inner, TILE), bf16),
            pltpu.VMEM((tokens, depth), bf16),
            pltpu.VMEM((tokens, owners * cap), bf16),
            pltpu.VMEM((owners, cap, depth), bf16),
            pltpu.VMEM((rows, depth), bf16),
            pltpu.VMEM((tiles, rows, TILE), f32),
            pltpu.VMEM((2, tiles, rows, TILE), bf16),
            pltpu.VMEM((2, tiles, rows, TILE), bf16),
            pltpu.VMEM((4, tiles, owners * cap, TILE), bf16),
            dma((4,)),
            dma((27,)), dma((27,)), dma((27,)), dma((27,)),
            dma((4,)), dma((4,)), dma((4,)), dma((4,)),
            dma((3,)), dma((3,)),
            dma((2, tiles, 8)), dma((4, tiles, owners)),
        ],
        compiler_params=pltpu.CompilerParams(
            collective_id=0, has_side_effects=True, vmem_limit_bytes=58 * 1024 * 1024
        ),
        name="moe_block",
    )(
        hidden_in.T,
        norm_gain.reshape(1, depth),
        expert_ids.T,
        gate_weights.T,
        jnp.swapaxes(gate_up_codes, 1, 2),
        jnp.swapaxes(gate_up_scales, 0, 1),
        down_codes,
        jnp.swapaxes(down_scales, 0, 1),
    )
    return out.T


def solution(mesh):
    placed = (
        P(("grp", "exp", "wsh"), None),
        P(),
        P(("grp", "exp", "wsh"), None),
        P(("grp", "exp", "wsh"), None),
        P("exp", None, "wsh"),
        P("exp", None, "wsh"),
        P("exp", None, "wsh"),
        P("exp", None, "wsh"),
    )
    body = per_device
    if mesh.shape["wsh"] == 4 and mesh.shape["exp"] == 4 and mesh.shape["grp"] == 2:
        body = fused_device
    return jax.shard_map(
        body,
        mesh=mesh,
        in_specs=placed,
        out_specs=P(("grp", "exp", "wsh"), None),
        check_vma=False,
    )
```

```python
import jax
import jax.numpy as jnp
from jax import lax
from jax.experimental import pallas as pl
from jax.experimental.pallas import tpu as pltpu
from jax.sharding import PartitionSpec as P

EPSILON = 1e-05
SWISH_ALPHA = 1.702


def normalize(hidden_in, norm_gain):
    values = hidden_in.astype(jnp.float32)
    meansq = jnp.mean(values * values, axis=-1, keepdims=True)
    return (values * lax.rsqrt(meansq + EPSILON) * norm_gain).astype(jnp.bfloat16)


def expand_block(mantissa, exponent):
    groups = exponent.shape[-2]
    factor = jnp.exp2(-exponent.astype(jnp.float32)).astype(jnp.bfloat16)
    shaped = mantissa.reshape(
        mantissa.shape[:-2] + (groups, mantissa.shape[-2] // groups, mantissa.shape[-1])
    )
    return (shaped * factor[..., :, None, :]).reshape(mantissa.shape)


def activate(gate_up, inner_width):
    gate_part = gate_up[:, :inner_width]
    upward = gate_up[:, inner_width:]
    return ((upward + 1.0) * gate_part * jax.nn.sigmoid(SWISH_ALPHA * gate_part)).astype(
        jnp.bfloat16
    )


def block_slots(block_ids, expert_count, capacity):
    rows, picks = block_ids.shape
    labels = jnp.arange(expert_count, dtype=jnp.int32)
    onehot = (block_ids.reshape(rows * picks)[:, None] == labels[None, :]).astype(jnp.int32)
    earlier = jnp.cumsum(onehot, axis=0) - onehot
    ranking = jnp.sum(earlier * onehot, axis=1).reshape(rows, picks)
    return jnp.where(ranking < capacity, ranking, -1)


def per_device(
    hidden_in,
    norm_gain,
    expert_ids,
    gate_weights,
    gate_up_codes,
    gate_up_scales,
    down_codes,
    down_scales,
):
    normed = normalize(hidden_in, norm_gain)
    tok_rows, model_width = hidden_in.shape
    picks_per = expert_ids.shape[1]
    owners = lax.axis_size("exp")
    capacity = min(tok_rows // 2, tok_rows * picks_per // owners)
    slot_index = block_slots(expert_ids, owners, capacity)
    target = jnp.where(slot_index >= 0, expert_ids * capacity + slot_index, -1)
    positions = jnp.arange(owners * capacity, dtype=jnp.int32)
    matches = target[:, :, None] == positions[None, None, :]
    placing = jnp.any(matches, axis=1).astype(jnp.bfloat16)
    outgoing = jnp.einsum("ts,td->sd", placing, normed, preferred_element_type=jnp.float32).astype(
        jnp.bfloat16
    )
    outgoing = outgoing.reshape(owners, capacity, model_width)
    inner_width = down_codes.shape[1]
    arrived = lax.all_to_all(outgoing, "exp", split_axis=0, concat_axis=0, tiled=True)
    arrived = arrived.reshape(owners * capacity, model_width)
    shard_piece = lax.all_gather((gate_up_codes[0], gate_up_scales[0]), "wsh", axis=1, tiled=True)
    gate_up = jnp.dot(
        arrived, expand_block(shard_piece[0], shard_piece[1]), preferred_element_type=jnp.float32
    )
    hidden_act = activate(gate_up, inner_width)
    shard_piece = lax.all_gather((down_codes[0], down_scales[0]), "wsh", axis=1, tiled=True)
    expert_out = jnp.dot(
        hidden_act, expand_block(shard_piece[0], shard_piece[1]), preferred_element_type=jnp.float32
    )
    expert_rows = expert_out.astype(jnp.bfloat16).reshape(owners, capacity, model_width)
    came_back = lax.all_to_all(expert_rows, "exp", split_axis=0, concat_axis=0, tiled=True).reshape(
        owners * capacity, model_width
    )
    weighting = jnp.sum(
        jnp.where(matches, gate_weights[:, :, None], jnp.zeros((), jnp.bfloat16)), axis=1
    )
    mixture = jnp.dot(weighting, came_back, preferred_element_type=jnp.float32)
    return mixture.astype(jnp.bfloat16)


MESH = pl.DeviceIdType.MESH
TILE = 256
GROUP = 32


def fused_kernel(
    hid, gain, ids, gates, guc, gus, dnc, dns, out,
    stage_g, stage_d, wg, wd, nrm, weighting, og, xb, first, act, res, back,
    load_sem, xs, xr, ys, yr, zs, zr, cs, cr, act_s, act_r, rs, rr,
):
    grp = lax.axis_index("grp")
    z = lax.axis_index("exp")
    w = lax.axis_index("wsh")
    x = w // 2
    c = w % 2
    slot = z * 2 + c
    mate = x * 2 + (1 - c)
    across = (1 - x) * 2 + c
    depth = stage_g.shape[1]
    inner, width = stage_d.shape
    half_g, half_d = depth // 2, inner // 2
    per_g, per_d = 9, 5
    step_g, step_d = half_g // per_g, half_d // per_d
    count_g = 3 * per_g
    count = count_g + 3 * per_d
    tokens = hid.shape[1]
    cap = og.shape[1]

    loads = []
    for j in range(3):
        rows = pl.ds(j * TILE, min(TILE, width - j * TILE))
        loads.append(pltpu.make_async_copy(guc.at[0, rows], stage_g.at[rows], load_sem.at[j]))
    loads.append(pltpu.make_async_copy(dnc.at[0], stage_d, load_sem.at[3]))
    for load in loads:
        load.start()

    barrier = pltpu.get_barrier_semaphore()
    pl.semaphore_signal(barrier, inc=1, device_id={"wsh": across}, device_id_type=MESH)
    pl.semaphore_signal(barrier, inc=1, device_id={"grp": 1 - grp}, device_id_type=MESH)
    for d in range(1, 8):
        other = (slot + d) % 8
        pl.semaphore_signal(
            barrier, inc=1, device_id={"exp": other // 2, "wsh": x * 2 + other % 2}, device_id_type=MESH
        )

    wg[0, 2] = jnp.zeros((depth, TILE), jnp.bfloat16)
    wd[0, 2] = jnp.zeros((inner, TILE), jnp.bfloat16)
    stage_g[width:, :] = jnp.zeros((stage_g.shape[0] - width, depth), jnp.bfloat16)

    def factor(scales, at, j, lanes):
        scale = jnp.exp2(-scales[at, :, pl.ds(j * TILE, lanes)].astype(jnp.float32))
        return jnp.broadcast_to(scale, (GROUP, lanes)).astype(jnp.bfloat16)

    def expand_down(j):
        lanes = min(TILE, width - j * TILE)

        @pl.loop(0, inner // GROUP)
        def _(g):
            row = pl.multiple_of(g * GROUP, GROUP)
            wd[0, j, pl.ds(row, GROUP), pl.ds(0, lanes)] = stage_d[
                pl.ds(row, GROUP), pl.ds(j * TILE, lanes)
            ] * factor(dns, g, j, lanes)

    def expand_gate_up(j):
        lanes = min(TILE, width - j * TILE)

        def block(at, extent):
            codes = stage_g[pl.ds(j * TILE, TILE), pl.ds(at, extent)].T
            for g in range(extent // GROUP):
                part = codes[g * GROUP : (g + 1) * GROUP, :lanes]
                scale = factor(gus, at // GROUP + g, j, lanes)
                wg[0, j, pl.ds(at + g * GROUP, GROUP), pl.ds(0, lanes)] = part * scale

        @pl.loop(0, depth // 128)
        def _(b):
            block(pl.multiple_of(b * 128, 128), 128)

        if depth % 128:
            block(depth // 128 * 128, depth % 128)

    def place(i):
        if i < count_g:
            return wg, i // per_g, i % per_g, half_g, step_g
        i = i - count_g
        return wd, i // per_d, i % per_d, half_d, step_d

    def x_copy(i):
        buf, j, s, half, step = place(i)
        rows = pl.ds(pl.multiple_of(grp * half + s * step, 16), step)
        return pltpu.make_async_remote_copy(
            src_ref=buf.at[0, j, rows], dst_ref=buf.at[1, j, rows], send_sem=xs.at[i], recv_sem=xr.at[i],
            device_id={"wsh": across}, device_id_type=MESH,
        )

    def y_copy(i, side=None):
        buf, j, s, half, step = place(i)
        side = grp if side is None else side
        rows = pl.ds(pl.multiple_of(side * half + s * step, 16), step)
        return pltpu.make_async_remote_copy(
            src_ref=buf.at[1, j, rows], dst_ref=buf.at[1, j, rows], send_sem=ys.at[i], recv_sem=yr.at[i],
            device_id={"grp": 1 - grp}, device_id_type=MESH,
        )

    def forward(i):
        x_copy(i).wait_recv()
        y_copy(i).start()

    def send_gate_up(j):
        loads[j].wait()
        expand_gate_up(j)
        if j == 0:
            pl.semaphore_wait(barrier, 9)
        for s in range(per_g):
            x_copy(j * per_g + s).start()

    send_gate_up(0)

    total = jnp.zeros((1, tokens), jnp.float32)
    for at in range(0, depth, 128):
        values = hid[at : min(at + 128, depth), :].astype(jnp.float32)
        total = total + jnp.sum(values * values, axis=0, keepdims=True)
    inverse = lax.rsqrt(total / depth + EPSILON)
    for at in range(0, depth, 128):
        end = min(at + 128, depth)
        values = (hid[at:end, :].astype(jnp.float32) * inverse).T
        nrm[:, at:end] = (values * gain[at:end].reshape(1, end - at)).astype(jnp.bfloat16)

    picks = ids.shape[0]
    owners = og.shape[0]
    chosen = ids[...]
    gate_values = gates[...].astype(jnp.float32)
    label = lax.broadcasted_iota(jnp.int32, (16, tokens), 0)
    named = jnp.zeros((16, tokens), jnp.float32)
    valued = jnp.zeros((16, tokens), jnp.float32)
    for k in range(picks):
        same = chosen[k : k + 1, :] == label
        named = named + jnp.where(same, 1.0, 0.0)
        valued = valued + jnp.where(same, gate_values[k : k + 1, :], 0.0)
    row_at = lax.broadcasted_iota(jnp.int32, (tokens, tokens), 0)
    col_at = lax.broadcasted_iota(jnp.int32, (tokens, tokens), 1)
    earlier = jnp.where(row_at < col_at, 1.0, 0.0).astype(jnp.bfloat16)
    rank = jnp.dot(named.astype(jnp.bfloat16), earlier, preferred_element_type=jnp.float32)
    position = lax.broadcasted_iota(jnp.int32, (cap, tokens), 0).astype(jnp.float32)
    placed = []
    for e in range(owners):
        hit = jnp.where(rank[e : e + 1, :] == position, named[e : e + 1, :], 0.0)
        placed.append(hit)
        og[e] = jnp.dot(
            hit.astype(jnp.bfloat16), nrm[...], preferred_element_type=jnp.float32
        ).astype(jnp.bfloat16)
    for pair in range(owners // 2):
        e = 2 * pair
        both = jnp.concatenate(
            [placed[e] * valued[e : e + 1, :], placed[e + 1] * valued[e + 1 : e + 2, :]], axis=0
        )
        weighting[:, 2 * cap * pair : 2 * cap * (pair + 1)] = both.T.astype(jnp.bfloat16)

    def slot_rows(s):
        return pl.ds(pl.multiple_of(s * cap, 16), cap)

    def z_copy(d):
        to = (z + d) % 4
        return pltpu.make_async_remote_copy(
            src_ref=og.at[to], dst_ref=xb.at[slot_rows(slot)], send_sem=zs.at[d], recv_sem=zr.at[d],
            device_id={"exp": to}, device_id_type=MESH,
        )

    def z_arrived(d):
        frm = ((z + 4 - d) % 4) * 2 + c
        pltpu.make_async_remote_copy(
            src_ref=og.at[0], dst_ref=xb.at[slot_rows(frm)], send_sem=zs.at[d], recv_sem=zr.at[d],
            device_id={"exp": (z + d) % 4}, device_id_type=MESH,
        ).wait_recv()

    def c_copy(d, core=None):
        core = c if core is None else core
        rows = slot_rows(((z + 4 - d) % 4) * 2 + core)
        return pltpu.make_async_remote_copy(
            src_ref=xb.at[rows], dst_ref=xb.at[rows], send_sem=cs.at[d], recv_sem=cr.at[d],
            device_id={"wsh": mate}, device_id_type=MESH,
        )

    for d in (2, 1, 3):
        z_copy(d).start()
    xb[slot_rows(slot), :] = og[z]
    c_copy(0).start()

    forward(0)
    send_gate_up(1)
    forward(1)
    send_gate_up(2)
    forward(2)
    loads[3].wait()
    for j in range(3):
        expand_down(j)
        for s in range(per_d):
            x_copy(count_g + j * per_d + s).start()
        forward(3 + j)
    for i in range(6, 21):
        forward(i)
    for d in (1, 3, 2):
        z_arrived(d)
        c_copy(d).start()
    forward(21)
    for d in range(4):
        c_copy(d, 1 - c).wait_recv()

    def a_copy(core, j):
        return pltpu.make_async_remote_copy(
            src_ref=act.at[core, j], dst_ref=act.at[core, j], send_sem=act_s.at[j], recv_sem=act_r.at[j],
            device_id={"wsh": mate}, device_id_type=MESH,
        )

    def activate_tile(j):
        for s in range(per_g):
            y_copy(j * per_g + s, 1 - grp).wait_recv()
        second = jnp.dot(xb[...], wg[1, j], preferred_element_type=jnp.float32)
        mine = first[j]
        gate = jnp.where(x == 0, mine, second)
        up = jnp.where(x == 0, second, mine)
        act[c, j] = ((up + 1.0) * gate * jax.nn.sigmoid(SWISH_ALPHA * gate)).astype(jnp.bfloat16)
        a_copy(c, j).start()

    for j in range(3):
        first[j] = jnp.dot(xb[...], wg[0, j], preferred_element_type=jnp.float32)
        forward(22 + j)
    activate_tile(0)
    forward(25)
    activate_tile(1)
    forward(26)
    forward(27)
    activate_tile(2)
    forward(28)
    for j in range(3):
        a_copy(1 - c, j).wait_recv()

    def quarter(h, core):
        return (x if h == 0 else 1 - x) * 2 + core

    def r_copy(h, j, d):
        other = (slot + d) % 8
        q = quarter(h, c)
        return pltpu.make_async_remote_copy(
            src_ref=res.at[h, j, slot_rows(other)], dst_ref=back.at[q, j, slot_rows(z)],
            send_sem=rs.at[h, j, d], recv_sem=rr.at[q, j, z],
            device_id={"exp": other // 2, "wsh": x * 2 + other % 2}, device_id_type=MESH,
        )

    def project(h, j):
        total = jnp.zeros((act.shape[2], TILE), jnp.float32)
        for core in range(2):
            for k in range(3):
                lanes = min(TILE, width - k * TILE)
                at = core * half_d + k * TILE
                total = total + jnp.dot(
                    act[core, k, :, :lanes], wd[h, j, at : at + lanes], preferred_element_type=jnp.float32
                )
        res[h, j] = total.astype(jnp.bfloat16)
        for d in (4, 5, 2, 3, 6, 7, 1):
            r_copy(h, j, d).start()
        back[quarter(h, c), j, slot_rows(z), :] = res[h, j, slot_rows(slot), :]

    def combine(h, j):
        for core in range(2):
            q = quarter(h, core)
            for e in range(4):
                @pl.when(jnp.logical_or(core != c, e != z))
                def _():
                    pltpu.make_async_remote_copy(
                        src_ref=res.at[h, j, slot_rows(0)], dst_ref=back.at[q, j, slot_rows(e)],
                        send_sem=rs.at[h, j, 1], recv_sem=rr.at[q, j, e],
                        device_id={"wsh": mate}, device_id_type=MESH,
                    ).wait_recv()
            mixed = jnp.dot(weighting[...], back[q, j], preferred_element_type=jnp.float32)
            lanes = min(TILE, width - j * TILE)
            at = pl.multiple_of(q * width + j * TILE, 16)
            out[pl.ds(at, lanes), :] = mixed.T[:lanes].astype(jnp.bfloat16)

    for j in range(3):
        project(0, j)
        forward(29 + j)
    for j in range(3):
        for i in range(max(32, count_g + per_d * j), count_g + per_d * (j + 1)):
            forward(i)
        for s in range(per_d):
            y_copy(count_g + j * per_d + s, 1 - grp).wait_recv()
        project(1, j)
    for j in range(3):
        combine(0, j)
    for j in range(3):
        combine(1, j)

    for i in range(count):
        x_copy(i).wait_send()
        y_copy(i).wait_send()
    for d in range(4):
        if d > 0:
            z_copy(d).wait_send()
        c_copy(d).wait_send()
    for j in range(3):
        a_copy(c, j).wait_send()
    for h in range(2):
        for j in range(3):
            for d in range(1, 8):
                r_copy(h, j, d).wait_send()


def fused_device(
    hidden_in,
    norm_gain,
    expert_ids,
    gate_weights,
    gate_up_codes,
    gate_up_scales,
    down_codes,
    down_scales,
):
    tokens, depth = hidden_in.shape
    width = gate_up_codes.shape[2]
    inner = down_codes.shape[1]
    owners = lax.axis_size("exp")
    cap = min(tokens // 2, tokens * expert_ids.shape[1] // owners)
    rows = 2 * owners * cap
    vmem = pl.BlockSpec(memory_space=pltpu.VMEM)
    hbm = pl.BlockSpec(memory_space=pl.ANY)
    bf16, f32 = jnp.bfloat16, jnp.float32
    dma = pltpu.SemaphoreType.DMA
    tiles = pl.cdiv(width, TILE)
    out = pl.pallas_call(
        fused_kernel,
        out_shape=jax.ShapeDtypeStruct((depth, tokens), bf16),
        in_specs=[vmem, vmem, vmem, vmem, hbm, vmem, hbm, vmem],
        out_specs=vmem,
        scratch_shapes=[
            pltpu.VMEM((tiles * TILE, depth), bf16),
            pltpu.VMEM((inner, width), bf16),
            pltpu.VMEM((2, tiles, depth, TILE), bf16),
            pltpu.VMEM((2, tiles, inner, TILE), bf16),
            pltpu.VMEM((tokens, depth), bf16),
            pltpu.VMEM((tokens, owners * cap), bf16),
            pltpu.VMEM((owners, cap, depth), bf16),
            pltpu.VMEM((rows, depth), bf16),
            pltpu.VMEM((tiles, rows, TILE), f32),
            pltpu.VMEM((2, tiles, rows, TILE), bf16),
            pltpu.VMEM((2, tiles, rows, TILE), bf16),
            pltpu.VMEM((4, tiles, owners * cap, TILE), bf16),
            dma((4,)),
            dma((42,)), dma((42,)), dma((42,)), dma((42,)),
            dma((4,)), dma((4,)), dma((4,)), dma((4,)),
            dma((3,)), dma((3,)),
            dma((2, tiles, 8)), dma((4, tiles, owners)),
        ],
        compiler_params=pltpu.CompilerParams(
            collective_id=0, has_side_effects=True, vmem_limit_bytes=58 * 1024 * 1024
        ),
        name="moe_block",
    )(
        hidden_in.T,
        norm_gain,
        expert_ids.T,
        gate_weights.T,
        jnp.swapaxes(gate_up_codes, 1, 2),
        jnp.swapaxes(gate_up_scales, 0, 1),
        down_codes,
        jnp.swapaxes(down_scales, 0, 1),
    )
    return out.T


def solution(mesh):
    placed = (
        P(("grp", "exp", "wsh"), None),
        P(),
        P(("grp", "exp", "wsh"), None),
        P(("grp", "exp", "wsh"), None),
        P("exp", None, "wsh"),
        P("exp", None, "wsh"),
        P("exp", None, "wsh"),
        P("exp", None, "wsh"),
    )
    body = per_device
    if mesh.shape["wsh"] == 4 and mesh.shape["exp"] == 4 and mesh.shape["grp"] == 2:
        body = fused_device
    return jax.shard_map(
        body,
        mesh=mesh,
        in_specs=placed,
        out_specs=P(("grp", "exp", "wsh"), None),
        check_vma=False,
    )
```

```python
import jax
import jax.numpy as jnp
from jax import lax
from jax.experimental import pallas as pl
from jax.experimental.pallas import tpu as pltpu
from jax.sharding import PartitionSpec as P

EPSILON = 1e-05
SWISH_ALPHA = 1.702


def normalize(hidden_in, norm_gain):
    values = hidden_in.astype(jnp.float32)
    meansq = jnp.mean(values * values, axis=-1, keepdims=True)
    return (values * lax.rsqrt(meansq + EPSILON) * norm_gain).astype(jnp.bfloat16)


def expand_block(mantissa, exponent):
    groups = exponent.shape[-2]
    factor = jnp.exp2(-exponent.astype(jnp.float32)).astype(jnp.bfloat16)
    shaped = mantissa.reshape(
        mantissa.shape[:-2] + (groups, mantissa.shape[-2] // groups, mantissa.shape[-1])
    )
    return (shaped * factor[..., :, None, :]).reshape(mantissa.shape)


def activate(gate_up, inner_width):
    gate_part = gate_up[:, :inner_width]
    upward = gate_up[:, inner_width:]
    return ((upward + 1.0) * gate_part * jax.nn.sigmoid(SWISH_ALPHA * gate_part)).astype(
        jnp.bfloat16
    )


def block_slots(block_ids, expert_count, capacity):
    rows, picks = block_ids.shape
    labels = jnp.arange(expert_count, dtype=jnp.int32)
    onehot = (block_ids.reshape(rows * picks)[:, None] == labels[None, :]).astype(jnp.int32)
    earlier = jnp.cumsum(onehot, axis=0) - onehot
    ranking = jnp.sum(earlier * onehot, axis=1).reshape(rows, picks)
    return jnp.where(ranking < capacity, ranking, -1)


def per_device(
    hidden_in,
    norm_gain,
    expert_ids,
    gate_weights,
    gate_up_codes,
    gate_up_scales,
    down_codes,
    down_scales,
):
    normed = normalize(hidden_in, norm_gain)
    tok_rows, model_width = hidden_in.shape
    picks_per = expert_ids.shape[1]
    owners = lax.axis_size("exp")
    capacity = min(tok_rows // 2, tok_rows * picks_per // owners)
    slot_index = block_slots(expert_ids, owners, capacity)
    target = jnp.where(slot_index >= 0, expert_ids * capacity + slot_index, -1)
    positions = jnp.arange(owners * capacity, dtype=jnp.int32)
    matches = target[:, :, None] == positions[None, None, :]
    placing = jnp.any(matches, axis=1).astype(jnp.bfloat16)
    outgoing = jnp.einsum("ts,td->sd", placing, normed, preferred_element_type=jnp.float32).astype(
        jnp.bfloat16
    )
    outgoing = outgoing.reshape(owners, capacity, model_width)
    inner_width = down_codes.shape[1]
    arrived = lax.all_to_all(outgoing, "exp", split_axis=0, concat_axis=0, tiled=True)
    arrived = arrived.reshape(owners * capacity, model_width)
    shard_piece = lax.all_gather((gate_up_codes[0], gate_up_scales[0]), "wsh", axis=1, tiled=True)
    gate_up = jnp.dot(
        arrived, expand_block(shard_piece[0], shard_piece[1]), preferred_element_type=jnp.float32
    )
    hidden_act = activate(gate_up, inner_width)
    shard_piece = lax.all_gather((down_codes[0], down_scales[0]), "wsh", axis=1, tiled=True)
    expert_out = jnp.dot(
        hidden_act, expand_block(shard_piece[0], shard_piece[1]), preferred_element_type=jnp.float32
    )
    expert_rows = expert_out.astype(jnp.bfloat16).reshape(owners, capacity, model_width)
    came_back = lax.all_to_all(expert_rows, "exp", split_axis=0, concat_axis=0, tiled=True).reshape(
        owners * capacity, model_width
    )
    weighting = jnp.sum(
        jnp.where(matches, gate_weights[:, :, None], jnp.zeros((), jnp.bfloat16)), axis=1
    )
    mixture = jnp.dot(weighting, came_back, preferred_element_type=jnp.float32)
    return mixture.astype(jnp.bfloat16)


MESH = pl.DeviceIdType.MESH
TILE = 256
GROUP = 32


def fused_kernel(
    hid, gain, ids, gates, guc, gus, dnc, dns, out,
    stage_g, stage_d, wg, wd, og, xb, first, act, res, far, summed, back,
    load_sem, xs, xr, ys, yr, zs, zr, cs, cr, act_s, act_r, rs, rr, fs, fr, ms,
):
    grp = lax.axis_index("grp")
    z = lax.axis_index("exp")
    w = lax.axis_index("wsh")
    x = w // 2
    c = w % 2
    slot = z * 2 + c
    mate = x * 2 + (1 - c)
    across = (1 - x) * 2 + c
    depth = stage_g.shape[1]
    inner, width = stage_d.shape
    half_g, half_d = depth // 2, inner // 2
    per_g, per_d = 9, 5
    step_g, step_d = half_g // per_g, half_d // per_d
    count_g = 3 * per_g
    count = count_g + 3 * per_d
    tokens = hid.shape[1]
    cap = og.shape[1]

    loads = []
    for j in range(3):
        rows = pl.ds(j * TILE, min(TILE, width - j * TILE))
        loads.append(pltpu.make_async_copy(guc.at[0, rows], stage_g.at[rows], load_sem.at[j]))
    loads.append(pltpu.make_async_copy(dnc.at[0], stage_d, load_sem.at[3]))
    for load in loads:
        load.start()

    barrier = pltpu.get_barrier_semaphore()
    pl.semaphore_signal(barrier, inc=1, device_id={"wsh": across}, device_id_type=MESH)
    pl.semaphore_signal(barrier, inc=1, device_id={"grp": 1 - grp}, device_id_type=MESH)
    for d in range(1, 8):
        other = (slot + d) % 8
        pl.semaphore_signal(
            barrier, inc=1, device_id={"exp": other // 2, "wsh": x * 2 + other % 2}, device_id_type=MESH
        )

    wg[0, 2] = jnp.zeros((depth, TILE), jnp.bfloat16)
    wd[0, 2] = jnp.zeros((inner, TILE), jnp.bfloat16)
    stage_g[width:, :] = jnp.zeros((stage_g.shape[0] - width, depth), jnp.bfloat16)

    def factor(scales, at, j, lanes):
        scale = jnp.exp2(-scales[at, :, pl.ds(j * TILE, lanes)].astype(jnp.float32))
        return jnp.broadcast_to(scale, (GROUP, lanes)).astype(jnp.bfloat16)

    def expand_down(j):
        lanes = min(TILE, width - j * TILE)

        @pl.loop(0, inner // GROUP)
        def _(g):
            row = pl.multiple_of(g * GROUP, GROUP)
            wd[0, j, pl.ds(row, GROUP), pl.ds(0, lanes)] = stage_d[
                pl.ds(row, GROUP), pl.ds(j * TILE, lanes)
            ] * factor(dns, g, j, lanes)

    def expand_gate_up(j):
        lanes = min(TILE, width - j * TILE)

        def block(at, extent):
            codes = stage_g[pl.ds(j * TILE, TILE), pl.ds(at, extent)].T
            for g in range(extent // GROUP):
                part = codes[g * GROUP : (g + 1) * GROUP, :lanes]
                scale = factor(gus, at // GROUP + g, j, lanes)
                wg[0, j, pl.ds(at + g * GROUP, GROUP), pl.ds(0, lanes)] = part * scale

        @pl.loop(0, depth // 128)
        def _(b):
            block(pl.multiple_of(b * 128, 128), 128)

        if depth % 128:
            block(depth // 128 * 128, depth % 128)

    def place(i):
        if i < count_g:
            return wg, i // per_g, i % per_g, half_g, step_g
        i = i - count_g
        return wd, i // per_d, i % per_d, half_d, step_d

    def x_copy(i):
        buf, j, s, half, step = place(i)
        rows = pl.ds(pl.multiple_of(grp * half + s * step, 16), step)
        return pltpu.make_async_remote_copy(
            src_ref=buf.at[0, j, rows], dst_ref=buf.at[1, j, rows], send_sem=xs.at[i], recv_sem=xr.at[i],
            device_id={"wsh": across}, device_id_type=MESH,
        )

    def y_copy(i, side=None):
        buf, j, s, half, step = place(i)
        side = grp if side is None else side
        rows = pl.ds(pl.multiple_of(side * half + s * step, 16), step)
        return pltpu.make_async_remote_copy(
            src_ref=buf.at[1, j, rows], dst_ref=buf.at[1, j, rows], send_sem=ys.at[i], recv_sem=yr.at[i],
            device_id={"grp": 1 - grp}, device_id_type=MESH,
        )

    def forward(i):
        x_copy(i).wait_recv()
        y_copy(i).start()

    def send_gate_up(j):
        loads[j].wait()
        expand_gate_up(j)
        if j == 0:
            pl.semaphore_wait(barrier, 9)
        for s in range(per_g):
            x_copy(j * per_g + s).start()

    send_gate_up(0)

    total = jnp.zeros((1, tokens), jnp.float32)
    for at in range(0, depth, 128):
        values = hid[at : min(at + 128, depth), :].astype(jnp.float32)
        total = total + jnp.sum(values * values, axis=0, keepdims=True)
    inverse = lax.rsqrt(total / depth + EPSILON)
    owners = og.shape[0]
    for at in range(0, depth, 128):
        end = min(at + 128, depth)
        values = (hid[at:end, :].astype(jnp.float32) * inverse).T[:cap]
        rows = (values * gain[at:end].reshape(1, end - at)).astype(jnp.bfloat16)
        for e in range(owners):
            og[e, :, at:end] = rows

    picks = ids.shape[0]
    chosen = ids[...]
    gate_values = gates[...].astype(jnp.float32)
    label = lax.broadcasted_iota(jnp.int32, (tokens, tokens), 0)
    valued = jnp.zeros((tokens, tokens), jnp.float32)
    for k in range(picks):
        valued = valued + jnp.where(chosen[k : k + 1, :] == label, gate_values[k : k + 1, :], 0.0)
    valued = valued.T
    spare = og.shape[2] - 128
    for e in range(owners):
        og[e, :, spare:] = jnp.broadcast_to(valued[:cap, e : e + 1], (cap, 128)).astype(jnp.bfloat16)

    def slot_rows(s):
        return pl.ds(pl.multiple_of(s * cap, 16), cap)

    def z_copy(d):
        to = (z + d) % 4
        return pltpu.make_async_remote_copy(
            src_ref=og.at[to], dst_ref=xb.at[slot_rows(slot)], send_sem=zs.at[d], recv_sem=zr.at[d],
            device_id={"exp": to}, device_id_type=MESH,
        )

    def z_arrived(d):
        frm = ((z + 4 - d) % 4) * 2 + c
        pltpu.make_async_remote_copy(
            src_ref=og.at[0], dst_ref=xb.at[slot_rows(frm)], send_sem=zs.at[d], recv_sem=zr.at[d],
            device_id={"exp": (z + d) % 4}, device_id_type=MESH,
        ).wait_recv()

    def c_copy(d, core=None):
        core = c if core is None else core
        rows = slot_rows(((z + 4 - d) % 4) * 2 + core)
        return pltpu.make_async_remote_copy(
            src_ref=xb.at[rows], dst_ref=xb.at[rows], send_sem=cs.at[d], recv_sem=cr.at[d],
            device_id={"wsh": mate}, device_id_type=MESH,
        )

    for d in (2, 1, 3):
        z_copy(d).start()
    xb[slot_rows(slot), :] = og[z]
    c_copy(0).start()

    forward(0)
    send_gate_up(1)
    forward(1)
    send_gate_up(2)
    forward(2)
    loads[3].wait()
    for j in range(3):
        expand_down(j)
        for s in range(per_d):
            x_copy(count_g + j * per_d + s).start()
        forward(3 + j)
    for i in range(6, 21):
        forward(i)
    for d in (1, 3, 2):
        z_arrived(d)
        c_copy(d).start()
    forward(21)
    for d in range(4):
        c_copy(d, 1 - c).wait_recv()

    def a_copy(core, j):
        return pltpu.make_async_remote_copy(
            src_ref=act.at[core, j], dst_ref=act.at[core, j], send_sem=act_s.at[j], recv_sem=act_r.at[j],
            device_id={"wsh": mate}, device_id_type=MESH,
        )

    def activate_tile(j):
        for s in range(per_g):
            y_copy(j * per_g + s, 1 - grp).wait_recv()
        if j == 2:
            forward(28)
        second = jnp.dot(xb[:, :depth], wg[1, j], preferred_element_type=jnp.float32)
        mine = first[j]
        gate = jnp.where(x == 0, mine, second)
        up = jnp.where(x == 0, second, mine)
        act[c, j] = ((up + 1.0) * gate * jax.nn.sigmoid(SWISH_ALPHA * gate)).astype(jnp.bfloat16)
        a_copy(c, j).start()

    for j in range(3):
        first[j] = jnp.dot(xb[:, :depth], wg[0, j], preferred_element_type=jnp.float32)
        forward(22 + j)
    activate_tile(0)
    forward(25)
    activate_tile(1)
    forward(26)
    forward(27)
    activate_tile(2)
    forward(29)
    for j in range(3):
        a_copy(1 - c, j).wait_recv()

    def quarter(h, core):
        return (x if h == 0 else 1 - x) * 2 + core

    pair = z + 1 - 2 * (z % 2)
    far_slot = jnp.where(z < 2, 4, 0)
    is_end = jnp.logical_or(z == 0, z == owners - 1)
    far_rows = pl.ds(pl.multiple_of(far_slot * cap, 16), 4 * cap)

    def near_copy(h, j, k):
        core = 1 - c if k == 0 else k - 1
        to = z if k == 0 else pair
        q, place_at = quarter(h, c), 0 if k == 0 else 1
        return pltpu.make_async_remote_copy(
            src_ref=res.at[h, j, slot_rows(to * 2 + core)], dst_ref=back.at[q, j, place_at],
            send_sem=rs.at[h, j, k], recv_sem=rr.at[q, j, place_at],
            device_id={"exp": to, "wsh": x * 2 + core}, device_id_type=MESH,
        )

    def far_copy(h, j):
        return pltpu.make_async_remote_copy(
            src_ref=res.at[h, j, far_rows], dst_ref=far.at[h, j], send_sem=fs.at[h, j], recv_sem=fr.at[h, j],
            device_id={"exp": pair}, device_id_type=MESH,
        )

    def sum_copy(h, j, k):
        to = far_slot // 2 + k // 2
        q = quarter(h, c)
        return pltpu.make_async_remote_copy(
            src_ref=summed.at[h, j, pl.ds(k * cap, cap)], dst_ref=back.at[q, j, 2],
            send_sem=ms.at[h, j, k], recv_sem=rr.at[q, j, 2],
            device_id={"exp": to, "wsh": x * 2 + k % 2}, device_id_type=MESH,
        )

    def merge(h, j):
        @pl.when(jnp.logical_not(is_end))
        def _():
            far_copy(h, j).wait_recv()
            own = res[h, j, far_rows, :].astype(jnp.float32)
            summed[h, j] = (own + far[h, j].astype(jnp.float32)).astype(jnp.bfloat16)
            for k in range(4):
                sum_copy(h, j, k).start()

    def project(h, j):
        total = jnp.zeros((act.shape[2], TILE), jnp.float32)
        for core in range(2):
            for k in range(3):
                lanes = min(TILE, width - k * TILE)
                at = core * half_d + k * TILE
                total = total + jnp.dot(
                    act[core, k, :, :lanes], wd[h, j, at : at + lanes], preferred_element_type=jnp.float32
                )
        weight = xb[:, spare : spare + 1].astype(jnp.float32)
        res[h, j] = (total.astype(jnp.bfloat16).astype(jnp.float32) * weight).astype(jnp.bfloat16)

        @pl.when(is_end)
        def _():
            far_copy(h, j).start()

        for k in (1, 2, 0):
            near_copy(h, j, k).start()
        back[quarter(h, c), j, 0] = res[h, j, slot_rows(slot), :]

    def combine(h, j):
        for core in range(2):
            q = quarter(h, core)

            def landed(k):
                pltpu.make_async_remote_copy(
                    src_ref=res.at[h, j, slot_rows(0)], dst_ref=back.at[q, j, k], send_sem=rs.at[h, j, 0],
                    recv_sem=rr.at[q, j, k], device_id={"wsh": mate}, device_id_type=MESH,
                ).wait_recv()

            @pl.when(core != c)
            def _():
                landed(0)

            landed(1)
            landed(2)
            mixed = back[q, j, 0].astype(jnp.float32) + back[q, j, 1].astype(jnp.float32)
            mixed = mixed + back[q, j, 2].astype(jnp.float32)
            lanes = min(TILE, width - j * TILE)
            at = pl.multiple_of(q * width + j * TILE, 16)
            mixed = jnp.concatenate([mixed, jnp.zeros((tokens - cap, TILE), jnp.float32)], axis=0)
            out[pl.ds(at, lanes), :] = mixed.T[:lanes].astype(jnp.bfloat16)

    forward(30)
    for j in range(3):
        project(0, j)
        forward(31 + j)
    forward(34)
    merge(0, 0)
    forward(35)
    for s in range(per_d):
        y_copy(count_g + s, 1 - grp).wait_recv()
    project(1, 0)
    forward(36)
    merge(0, 1)
    for i in range(37, 40):
        forward(i)
    merge(0, 2)
    for s in range(per_d):
        y_copy(count_g + per_d + s, 1 - grp).wait_recv()
    forward(40)
    project(1, 1)
    forward(41)
    merge(1, 0)
    combine(0, 0)
    for s in range(per_d):
        y_copy(count_g + 2 * per_d + s, 1 - grp).wait_recv()
    project(1, 2)
    merge(1, 1)
    combine(0, 1)
    combine(0, 2)
    merge(1, 2)
    for j in range(3):
        combine(1, j)

    for i in range(count):
        x_copy(i).wait_send()
        y_copy(i).wait_send()
    for d in range(4):
        if d > 0:
            z_copy(d).wait_send()
        c_copy(d).wait_send()
    for j in range(3):
        a_copy(c, j).wait_send()
    for h in range(2):
        for j in range(3):
            for k in range(3):
                near_copy(h, j, k).wait_send()

            @pl.when(is_end)
            def _():
                far_copy(h, j).wait_send()

            @pl.when(jnp.logical_not(is_end))
            def _():
                for k in range(4):
                    sum_copy(h, j, k).wait_send()


def fused_device(
    hidden_in,
    norm_gain,
    expert_ids,
    gate_weights,
    gate_up_codes,
    gate_up_scales,
    down_codes,
    down_scales,
):
    tokens, depth = hidden_in.shape
    width = gate_up_codes.shape[2]
    inner = down_codes.shape[1]
    owners = lax.axis_size("exp")
    cap = min(tokens // 2, tokens * expert_ids.shape[1] // owners)
    if expert_ids.shape[1] != owners:
        return per_device(
            hidden_in, norm_gain, expert_ids, gate_weights,
            gate_up_codes, gate_up_scales, down_codes, down_scales,
        )
    rows = 2 * owners * cap
    span = (pl.cdiv(depth, 128) + 1) * 128
    vmem = pl.BlockSpec(memory_space=pltpu.VMEM)
    hbm = pl.BlockSpec(memory_space=pl.ANY)
    bf16, f32 = jnp.bfloat16, jnp.float32
    dma = pltpu.SemaphoreType.DMA
    tiles = pl.cdiv(width, TILE)
    out = pl.pallas_call(
        fused_kernel,
        out_shape=jax.ShapeDtypeStruct((depth, tokens), bf16),
        in_specs=[vmem, vmem, vmem, vmem, hbm, vmem, hbm, vmem],
        out_specs=vmem,
        scratch_shapes=[
            pltpu.VMEM((tiles * TILE, depth), bf16),
            pltpu.VMEM((inner, width), bf16),
            pltpu.VMEM((2, tiles, depth, TILE), bf16),
            pltpu.VMEM((2, tiles, inner, TILE), bf16),
            pltpu.VMEM((owners, cap, span), bf16),
            pltpu.VMEM((rows, span), bf16),
            pltpu.VMEM((tiles, rows, TILE), f32),
            pltpu.VMEM((2, tiles, rows, TILE), bf16),
            pltpu.VMEM((2, tiles, rows, TILE), bf16),
            pltpu.VMEM((2, tiles, rows // 2, TILE), bf16),
            pltpu.VMEM((2, tiles, rows // 2, TILE), bf16),
            pltpu.VMEM((4, tiles, 3, cap, TILE), bf16),
            dma((4,)),
            dma((42,)), dma((42,)), dma((42,)), dma((42,)),
            dma((4,)), dma((4,)), dma((4,)), dma((4,)),
            dma((3,)), dma((3,)),
            dma((2, tiles, 3)), dma((4, tiles, 3)),
            dma((2, tiles)), dma((2, tiles)), dma((2, tiles, 4)),
        ],
        compiler_params=pltpu.CompilerParams(
            collective_id=0, has_side_effects=True, vmem_limit_bytes=58 * 1024 * 1024
        ),
        name="moe_block",
    )(
        hidden_in.T,
        norm_gain,
        expert_ids.T,
        gate_weights.T,
        jnp.swapaxes(gate_up_codes, 1, 2),
        jnp.swapaxes(gate_up_scales, 0, 1),
        down_codes,
        jnp.swapaxes(down_scales, 0, 1),
    )
    return out.T


def solution(mesh):
    placed = (
        P(("grp", "exp", "wsh"), None),
        P(),
        P(("grp", "exp", "wsh"), None),
        P(("grp", "exp", "wsh"), None),
        P("exp", None, "wsh"),
        P("exp", None, "wsh"),
        P("exp", None, "wsh"),
        P("exp", None, "wsh"),
    )
    body = per_device
    if mesh.shape["wsh"] == 4 and mesh.shape["exp"] == 4 and mesh.shape["grp"] == 2:
        body = fused_device
    return jax.shard_map(
        body,
        mesh=mesh,
        in_specs=placed,
        out_specs=P(("grp", "exp", "wsh"), None),
        check_vma=False,
    )
```

```python
import jax
import jax.numpy as jnp
from jax import lax
from jax.experimental import pallas as pl
from jax.experimental.pallas import tpu as pltpu
from jax.sharding import PartitionSpec as P

EPSILON = 1e-05
SWISH_ALPHA = 1.702


def normalize(hidden_in, norm_gain):
    values = hidden_in.astype(jnp.float32)
    meansq = jnp.mean(values * values, axis=-1, keepdims=True)
    return (values * lax.rsqrt(meansq + EPSILON) * norm_gain).astype(jnp.bfloat16)


def expand_block(mantissa, exponent):
    groups = exponent.shape[-2]
    factor = jnp.exp2(-exponent.astype(jnp.float32)).astype(jnp.bfloat16)
    shaped = mantissa.reshape(
        mantissa.shape[:-2] + (groups, mantissa.shape[-2] // groups, mantissa.shape[-1])
    )
    return (shaped * factor[..., :, None, :]).reshape(mantissa.shape)


def activate(gate_up, inner_width):
    gate_part = gate_up[:, :inner_width]
    upward = gate_up[:, inner_width:]
    return ((upward + 1.0) * gate_part * jax.nn.sigmoid(SWISH_ALPHA * gate_part)).astype(
        jnp.bfloat16
    )


def block_slots(block_ids, expert_count, capacity):
    rows, picks = block_ids.shape
    labels = jnp.arange(expert_count, dtype=jnp.int32)
    onehot = (block_ids.reshape(rows * picks)[:, None] == labels[None, :]).astype(jnp.int32)
    earlier = jnp.cumsum(onehot, axis=0) - onehot
    ranking = jnp.sum(earlier * onehot, axis=1).reshape(rows, picks)
    return jnp.where(ranking < capacity, ranking, -1)


def per_device(
    hidden_in,
    norm_gain,
    expert_ids,
    gate_weights,
    gate_up_codes,
    gate_up_scales,
    down_codes,
    down_scales,
):
    normed = normalize(hidden_in, norm_gain)
    tok_rows, model_width = hidden_in.shape
    picks_per = expert_ids.shape[1]
    owners = lax.axis_size("exp")
    capacity = min(tok_rows // 2, tok_rows * picks_per // owners)
    slot_index = block_slots(expert_ids, owners, capacity)
    target = jnp.where(slot_index >= 0, expert_ids * capacity + slot_index, -1)
    positions = jnp.arange(owners * capacity, dtype=jnp.int32)
    matches = target[:, :, None] == positions[None, None, :]
    placing = jnp.any(matches, axis=1).astype(jnp.bfloat16)
    outgoing = jnp.einsum("ts,td->sd", placing, normed, preferred_element_type=jnp.float32).astype(
        jnp.bfloat16
    )
    outgoing = outgoing.reshape(owners, capacity, model_width)
    inner_width = down_codes.shape[1]
    arrived = lax.all_to_all(outgoing, "exp", split_axis=0, concat_axis=0, tiled=True)
    arrived = arrived.reshape(owners * capacity, model_width)
    shard_piece = lax.all_gather((gate_up_codes[0], gate_up_scales[0]), "wsh", axis=1, tiled=True)
    gate_up = jnp.dot(
        arrived, expand_block(shard_piece[0], shard_piece[1]), preferred_element_type=jnp.float32
    )
    hidden_act = activate(gate_up, inner_width)
    shard_piece = lax.all_gather((down_codes[0], down_scales[0]), "wsh", axis=1, tiled=True)
    expert_out = jnp.dot(
        hidden_act, expand_block(shard_piece[0], shard_piece[1]), preferred_element_type=jnp.float32
    )
    expert_rows = expert_out.astype(jnp.bfloat16).reshape(owners, capacity, model_width)
    came_back = lax.all_to_all(expert_rows, "exp", split_axis=0, concat_axis=0, tiled=True).reshape(
        owners * capacity, model_width
    )
    weighting = jnp.sum(
        jnp.where(matches, gate_weights[:, :, None], jnp.zeros((), jnp.bfloat16)), axis=1
    )
    mixture = jnp.dot(weighting, came_back, preferred_element_type=jnp.float32)
    return mixture.astype(jnp.bfloat16)


MESH = pl.DeviceIdType.MESH
TILE = 256
GROUP = 32


def fused_kernel(
    hid, gain, ids, gates, guc, gus, dnc, dns, out,
    stage_g, stage_d, wg, wd, og, xb, first, act, res, far, summed, back,
    load_sem, xs, xr, ys, yr, zs, zr, cs, cr, act_s, act_r, rs, rr, fs, fr, ms,
):
    grp = lax.axis_index("grp")
    z = lax.axis_index("exp")
    w = lax.axis_index("wsh")
    x = w // 2
    c = w % 2
    slot = z * 2 + c
    mate = x * 2 + (1 - c)
    across = (1 - x) * 2 + c
    depth = stage_g.shape[1]
    inner, width = stage_d.shape
    half_g, half_d = depth // 2, inner // 2
    per_g, per_d = 9, 5
    step_g, step_d = half_g // per_g, half_d // per_d
    count_g = 3 * per_g
    count = count_g + 3 * per_d
    tokens = hid.shape[1]
    cap = og.shape[1]

    loads = []
    for j in range(3):
        rows = pl.ds(j * TILE, min(TILE, width - j * TILE))
        loads.append(pltpu.make_async_copy(guc.at[0, rows], stage_g.at[rows], load_sem.at[j]))
    loads.append(pltpu.make_async_copy(dnc.at[0], stage_d, load_sem.at[3]))
    for load in loads:
        load.start()

    barrier = pltpu.get_barrier_semaphore()
    pl.semaphore_signal(barrier, inc=1, device_id={"wsh": across}, device_id_type=MESH)
    pl.semaphore_signal(barrier, inc=1, device_id={"grp": 1 - grp}, device_id_type=MESH)
    for d in range(1, 8):
        other = (slot + d) % 8
        pl.semaphore_signal(
            barrier, inc=1, device_id={"exp": other // 2, "wsh": x * 2 + other % 2}, device_id_type=MESH
        )

    wg[0, 2] = jnp.zeros((depth, TILE), jnp.bfloat16)
    wd[0, 2] = jnp.zeros((inner, TILE), jnp.bfloat16)
    stage_g[width:, :] = jnp.zeros((stage_g.shape[0] - width, depth), jnp.bfloat16)

    def factor(scales, at, j, lanes):
        scale = jnp.exp2(-scales[at, :, pl.ds(j * TILE, lanes)].astype(jnp.float32))
        return jnp.broadcast_to(scale, (GROUP, lanes)).astype(jnp.bfloat16)

    def expand_down(j):
        lanes = min(TILE, width - j * TILE)

        @pl.loop(0, inner // GROUP)
        def _(g):
            row = pl.multiple_of(g * GROUP, GROUP)
            wd[0, j, pl.ds(row, GROUP), pl.ds(0, lanes)] = stage_d[
                pl.ds(row, GROUP), pl.ds(j * TILE, lanes)
            ] * factor(dns, g, j, lanes)

    def expand_gate_up(j):
        lanes = min(TILE, width - j * TILE)

        def block(at, extent):
            codes = stage_g[pl.ds(j * TILE, TILE), pl.ds(at, extent)].T
            for g in range(extent // GROUP):
                part = codes[g * GROUP : (g + 1) * GROUP, :lanes]
                scale = factor(gus, at // GROUP + g, j, lanes)
                wg[0, j, pl.ds(at + g * GROUP, GROUP), pl.ds(0, lanes)] = part * scale

        @pl.loop(0, depth // 128)
        def _(b):
            block(pl.multiple_of(b * 128, 128), 128)

        if depth % 128:
            block(depth // 128 * 128, depth % 128)

    def place(i):
        if i < count_g:
            return wg, i // per_g, i % per_g, half_g, step_g
        i = i - count_g
        return wd, i // per_d, i % per_d, half_d, step_d

    def x_copy(i):
        buf, j, s, half, step = place(i)
        rows = pl.ds(pl.multiple_of(grp * half + s * step, 16), step)
        return pltpu.make_async_remote_copy(
            src_ref=buf.at[0, j, rows], dst_ref=buf.at[1, j, rows], send_sem=xs.at[i], recv_sem=xr.at[i],
            device_id={"wsh": across}, device_id_type=MESH,
        )

    def y_copy(i, side=None):
        buf, j, s, half, step = place(i)
        side = grp if side is None else side
        rows = pl.ds(pl.multiple_of(side * half + s * step, 16), step)
        return pltpu.make_async_remote_copy(
            src_ref=buf.at[1, j, rows], dst_ref=buf.at[1, j, rows], send_sem=ys.at[i], recv_sem=yr.at[i],
            device_id={"grp": 1 - grp}, device_id_type=MESH,
        )

    def forward(i):
        x_copy(i).wait_recv()
        y_copy(i).start()

    def send_gate_up(j):
        loads[j].wait()
        expand_gate_up(j)
        if j == 0:
            pl.semaphore_wait(barrier, 9)
        for s in range(per_g):
            x_copy(j * per_g + s).start()

    send_gate_up(0)

    total = jnp.zeros((1, tokens), jnp.float32)
    for at in range(0, depth, 128):
        values = hid[at : min(at + 128, depth), :].astype(jnp.float32)
        total = total + jnp.sum(values * values, axis=0, keepdims=True)
    inverse = lax.rsqrt(total / depth + EPSILON)
    owners = og.shape[0]
    for at in range(0, depth, 128):
        end = min(at + 128, depth)
        values = (hid[at:end, :].astype(jnp.float32) * inverse).T[:cap]
        rows = (values * gain[at:end].reshape(1, end - at)).astype(jnp.bfloat16)
        for e in range(owners):
            og[e, :, at:end] = rows

    picks = ids.shape[0]
    chosen = ids[...]
    gate_values = gates[...].astype(jnp.float32)
    label = lax.broadcasted_iota(jnp.int32, (tokens, tokens), 0)
    valued = jnp.zeros((tokens, tokens), jnp.float32)
    for k in range(picks):
        valued = valued + jnp.where(chosen[k : k + 1, :] == label, gate_values[k : k + 1, :], 0.0)
    valued = valued.T
    spare = og.shape[2] - 128
    for e in range(owners):
        og[e, :, spare:] = jnp.broadcast_to(valued[:cap, e : e + 1], (cap, 128)).astype(jnp.bfloat16)

    def slot_rows(s):
        return pl.ds(pl.multiple_of(s * cap, 16), cap)

    def z_copy(d):
        to = (z + d) % 4
        return pltpu.make_async_remote_copy(
            src_ref=og.at[to], dst_ref=xb.at[slot_rows(slot)], send_sem=zs.at[d], recv_sem=zr.at[d],
            device_id={"exp": to}, device_id_type=MESH,
        )

    def z_arrived(d):
        frm = ((z + 4 - d) % 4) * 2 + c
        pltpu.make_async_remote_copy(
            src_ref=og.at[0], dst_ref=xb.at[slot_rows(frm)], send_sem=zs.at[d], recv_sem=zr.at[d],
            device_id={"exp": (z + d) % 4}, device_id_type=MESH,
        ).wait_recv()

    def c_copy(d, core=None):
        core = c if core is None else core
        rows = slot_rows(((z + 4 - d) % 4) * 2 + core)
        return pltpu.make_async_remote_copy(
            src_ref=xb.at[rows], dst_ref=xb.at[rows], send_sem=cs.at[d], recv_sem=cr.at[d],
            device_id={"wsh": mate}, device_id_type=MESH,
        )

    for d in (2, 1, 3):
        z_copy(d).start()
    xb[slot_rows(slot), :] = og[z]
    c_copy(0).start()

    forward(0)
    send_gate_up(1)
    forward(1)
    send_gate_up(2)
    forward(2)
    loads[3].wait()
    for j in range(3):
        expand_down(j)
        for s in range(per_d):
            x_copy(count_g + j * per_d + s).start()
        forward(3 + j)
    for i in range(6, 21):
        forward(i)
    for d in (1, 3, 2):
        z_arrived(d)
        c_copy(d).start()
    forward(21)
    for d in range(4):
        c_copy(d, 1 - c).wait_recv()

    def a_copy(core, j):
        return pltpu.make_async_remote_copy(
            src_ref=act.at[core, j], dst_ref=act.at[core, j], send_sem=act_s.at[j], recv_sem=act_r.at[j],
            device_id={"wsh": mate}, device_id_type=MESH,
        )

    def activate_tile(j):
        for s in range(per_g):
            y_copy(j * per_g + s, 1 - grp).wait_recv()
        if j == 2:
            forward(28)
        second = jnp.dot(xb[:, :depth], wg[1, j], preferred_element_type=jnp.float32)
        mine = first[j]
        gate = jnp.where(x == 0, mine, second)
        up = jnp.where(x == 0, second, mine)
        act[c, j] = ((up + 1.0) * gate * jax.nn.sigmoid(SWISH_ALPHA * gate)).astype(jnp.bfloat16)
        a_copy(c, j).start()

    for j in range(3):
        first[j] = jnp.dot(xb[:, :depth], wg[0, j], preferred_element_type=jnp.float32)
        forward(22 + j)
    activate_tile(0)
    forward(25)
    activate_tile(1)
    forward(26)
    forward(27)
    activate_tile(2)
    forward(29)
    for j in range(3):
        a_copy(1 - c, j).wait_recv()

    def quarter(h, core):
        return (x if h == 0 else 1 - x) * 2 + core

    pair = z + 1 - 2 * (z % 2)
    far_slot = jnp.where(z < 2, 4, 0)
    is_end = jnp.logical_or(z == 0, z == owners - 1)

    def near_copy(h, j, k):
        core = 1 - c if k == 0 else k - 1
        to = z if k == 0 else pair
        q, place_at = quarter(h, c), 0 if k == 0 else 1
        return pltpu.make_async_remote_copy(
            src_ref=res.at[h, j, slot_rows(to * 2 + core)], dst_ref=back.at[q, j, place_at],
            send_sem=rs.at[h, j, k], recv_sem=rr.at[q, j, place_at],
            device_id={"exp": to, "wsh": x * 2 + core}, device_id_type=MESH,
        )

    def far_copy(h, j, k):
        return pltpu.make_async_remote_copy(
            src_ref=res.at[h, j, slot_rows(far_slot + k)], dst_ref=far.at[h, j, pl.ds(k * cap, cap)],
            send_sem=fs.at[h, j, k], recv_sem=fr.at[h, j, k],
            device_id={"exp": pair}, device_id_type=MESH,
        )

    def sum_copy(h, j, k):
        to = far_slot // 2 + k // 2
        q = quarter(h, c)
        return pltpu.make_async_remote_copy(
            src_ref=summed.at[h, j, pl.ds(k * cap, cap)], dst_ref=back.at[q, j, 2],
            send_sem=ms.at[h, j, k], recv_sem=rr.at[q, j, 2],
            device_id={"exp": to, "wsh": x * 2 + k % 2}, device_id_type=MESH,
        )

    def merge(h, j):
        @pl.when(jnp.logical_not(is_end))
        def _():
            for k in range(4):
                rows = pl.ds(k * cap, cap)
                far_copy(h, j, k).wait_recv()
                own = res[h, j, slot_rows(far_slot + k), :].astype(jnp.float32)
                summed[h, j, rows, :] = (own + far[h, j, rows, :].astype(jnp.float32)).astype(jnp.bfloat16)
                sum_copy(h, j, k).start()

    def project(h, j):
        total = jnp.zeros((act.shape[2], TILE), jnp.float32)
        for core in range(2):
            for k in range(3):
                lanes = min(TILE, width - k * TILE)
                at = core * half_d + k * TILE
                total = total + jnp.dot(
                    act[core, k, :, :lanes], wd[h, j, at : at + lanes], preferred_element_type=jnp.float32
                )
        weight = xb[:, spare : spare + 1].astype(jnp.float32)
        res[h, j] = (total.astype(jnp.bfloat16).astype(jnp.float32) * weight).astype(jnp.bfloat16)

        @pl.when(is_end)
        def _():
            for k in range(4):
                far_copy(h, j, k).start()

        for k in (1, 2, 0):
            near_copy(h, j, k).start()
        back[quarter(h, c), j, 0] = res[h, j, slot_rows(slot), :]

    def combine(h, j):
        for core in range(2):
            q = quarter(h, core)

            def landed(k):
                pltpu.make_async_remote_copy(
                    src_ref=res.at[h, j, slot_rows(0)], dst_ref=back.at[q, j, k], send_sem=rs.at[h, j, 0],
                    recv_sem=rr.at[q, j, k], device_id={"wsh": mate}, device_id_type=MESH,
                ).wait_recv()

            @pl.when(core != c)
            def _():
                landed(0)

            landed(1)
            landed(2)
            mixed = back[q, j, 0].astype(jnp.float32) + back[q, j, 1].astype(jnp.float32)
            mixed = mixed + back[q, j, 2].astype(jnp.float32)
            lanes = min(TILE, width - j * TILE)
            at = pl.multiple_of(q * width + j * TILE, 16)
            mixed = jnp.concatenate([mixed, jnp.zeros((tokens - cap, TILE), jnp.float32)], axis=0)
            out[pl.ds(at, lanes), :] = mixed.T[:lanes].astype(jnp.bfloat16)

    forward(30)
    for j in range(3):
        project(0, j)
        forward(31 + j)
    forward(34)
    merge(0, 0)
    forward(35)
    for s in range(per_d):
        y_copy(count_g + s, 1 - grp).wait_recv()
    project(1, 0)
    forward(36)
    merge(0, 1)
    for i in range(37, 40):
        forward(i)
    merge(0, 2)
    for s in range(per_d):
        y_copy(count_g + per_d + s, 1 - grp).wait_recv()
    forward(40)
    project(1, 1)
    forward(41)
    merge(1, 0)
    combine(0, 0)
    for s in range(per_d):
        y_copy(count_g + 2 * per_d + s, 1 - grp).wait_recv()
    project(1, 2)
    merge(1, 1)
    combine(0, 1)
    combine(0, 2)
    merge(1, 2)
    for j in range(3):
        combine(1, j)

    for i in range(count):
        x_copy(i).wait_send()
        y_copy(i).wait_send()
    for d in range(4):
        if d > 0:
            z_copy(d).wait_send()
        c_copy(d).wait_send()
    for j in range(3):
        a_copy(c, j).wait_send()
    for h in range(2):
        for j in range(3):
            for k in range(3):
                near_copy(h, j, k).wait_send()

            @pl.when(is_end)
            def _():
                for k in range(4):
                    far_copy(h, j, k).wait_send()

            @pl.when(jnp.logical_not(is_end))
            def _():
                for k in range(4):
                    sum_copy(h, j, k).wait_send()


def fused_device(
    hidden_in,
    norm_gain,
    expert_ids,
    gate_weights,
    gate_up_codes,
    gate_up_scales,
    down_codes,
    down_scales,
):
    tokens, depth = hidden_in.shape
    width = gate_up_codes.shape[2]
    inner = down_codes.shape[1]
    owners = lax.axis_size("exp")
    cap = min(tokens // 2, tokens * expert_ids.shape[1] // owners)
    if expert_ids.shape[1] != owners:
        return per_device(
            hidden_in, norm_gain, expert_ids, gate_weights,
            gate_up_codes, gate_up_scales, down_codes, down_scales,
        )
    rows = 2 * owners * cap
    span = (pl.cdiv(depth, 128) + 1) * 128
    vmem = pl.BlockSpec(memory_space=pltpu.VMEM)
    hbm = pl.BlockSpec(memory_space=pl.ANY)
    bf16, f32 = jnp.bfloat16, jnp.float32
    dma = pltpu.SemaphoreType.DMA
    tiles = pl.cdiv(width, TILE)
    out = pl.pallas_call(
        fused_kernel,
        out_shape=jax.ShapeDtypeStruct((depth, tokens), bf16),
        in_specs=[vmem, vmem, vmem, vmem, hbm, vmem, hbm, vmem],
        out_specs=vmem,
        scratch_shapes=[
            pltpu.VMEM((tiles * TILE, depth), bf16),
            pltpu.VMEM((inner, width), bf16),
            pltpu.VMEM((2, tiles, depth, TILE), bf16),
            pltpu.VMEM((2, tiles, inner, TILE), bf16),
            pltpu.VMEM((owners, cap, span), bf16),
            pltpu.VMEM((rows, span), bf16),
            pltpu.VMEM((tiles, rows, TILE), f32),
            pltpu.VMEM((2, tiles, rows, TILE), bf16),
            pltpu.VMEM((2, tiles, rows, TILE), bf16),
            pltpu.VMEM((2, tiles, rows // 2, TILE), bf16),
            pltpu.VMEM((2, tiles, rows // 2, TILE), bf16),
            pltpu.VMEM((4, tiles, 3, cap, TILE), bf16),
            dma((4,)),
            dma((42,)), dma((42,)), dma((42,)), dma((42,)),
            dma((4,)), dma((4,)), dma((4,)), dma((4,)),
            dma((3,)), dma((3,)),
            dma((2, tiles, 3)), dma((4, tiles, 3)),
            dma((2, tiles, 4)), dma((2, tiles, 4)), dma((2, tiles, 4)),
        ],
        compiler_params=pltpu.CompilerParams(
            collective_id=0, has_side_effects=True, vmem_limit_bytes=58 * 1024 * 1024
        ),
        name="moe_block",
    )(
        hidden_in.T,
        norm_gain,
        expert_ids.T,
        gate_weights.T,
        jnp.swapaxes(gate_up_codes, 1, 2),
        jnp.swapaxes(gate_up_scales, 0, 1),
        down_codes,
        jnp.swapaxes(down_scales, 0, 1),
    )
    return out.T


def solution(mesh):
    placed = (
        P(("grp", "exp", "wsh"), None),
        P(),
        P(("grp", "exp", "wsh"), None),
        P(("grp", "exp", "wsh"), None),
        P("exp", None, "wsh"),
        P("exp", None, "wsh"),
        P("exp", None, "wsh"),
        P("exp", None, "wsh"),
    )
    body = per_device
    if mesh.shape["wsh"] == 4 and mesh.shape["exp"] == 4 and mesh.shape["grp"] == 2:
        body = fused_device
    return jax.shard_map(
        body,
        mesh=mesh,
        in_specs=placed,
        out_specs=P(("grp", "exp", "wsh"), None),
        check_vma=False,
    )
```
